256 devices in a mesh: row: 16 (over x, y), col: 16 (over z, core).
Axes of the slice: x: 4, y: 4, z: 8, core: 2. Of those that a mesh axis runs over, the one named last changes fastest.
Arguments:
- matrix: float32 [16384, 8192], P('row', 'col'), may hold values from -3 to 4, as said below
- pattern: int32 [2, 128], replicated, may hold values from 0 to 1, as said below
Outputs:
- panel: float32 [16384, 1024], P('row')
- schur: float32 [16384, 8192], P('row', 'col')
The draws below stay inside these ranges and needn't reach their ends.
Inputs may be any that keep to these rules, and one draw needn't show every extreme that they name: `matrix`: the leading square of order 2 * 4 * 128 in natural order is symmetric and each diagonal entry exceeds the sum of the magnitudes of the other entries of its row. pattern[1, g] is 1 wherever pattern[0, g] is 1; both are 1 for g below 8.
All inputs are finite; a program needn't handle non-finite values.
Results may differ from the reference program's by a relative error of at most 0.000057.
Values sent between devices are 32-bit elements; how exact they have to be, the bound alone decides.
No kernel may reach another device: no remote copies, remote signals or barrier semaphores. Data moves between devices by JAX's collectives and lax.ppermute only.
A program may use at most 128 MiB of HBM per device.

```python
import jax
import jax.numpy as jnp
from jax import lax

BLK = 128
PB = 4
RB = 8
CB = 4
NR = 128
NC = 64
N_ROW = 16
N_COL = 16


def draw_matrix(key, part):
    key = jax.random.fold_in(key, 7)
    key_base = jax.random.fold_in(key, 0)
    key_sym = jax.random.fold_in(key, 1)
    key_diag = jax.random.fold_in(key, 2)
    key_perm = jax.random.fold_in(key, 4)
    key_link = jax.random.fold_in(key, 5)
    total_rows = NR * BLK
    total_cols = NC * BLK
    panel_width = 2 * PB * BLK
    base = 0.5 * jax.random.normal(key_base, (total_rows, total_cols), jnp.float32)
    links = jax.random.uniform(key_link, (2, panel_width), jnp.float32, -0.7, 0.7)
    base = jnp.clip(base, -3.0, 3.0)
    first_perm = jax.random.permutation(jax.random.fold_in(key_perm, 1), panel_width)
    second_perm = jax.random.permutation(jax.random.fold_in(key_perm, 2), panel_width)
    columns = jnp.arange(panel_width)[None, :]
    linked = jnp.where(columns == first_perm[:, None], links[0][:, None], 0.0)
    linked = linked + jnp.where(columns == second_perm[:, None], links[1][:, None], 0.0)
    dense = jax.random.uniform(key_sym, (panel_width, panel_width), jnp.float32, -1.0, 1.0) * (0.3 / (panel_width - 1))
    coupling = dense + linked
    symmetric = 0.5 * (coupling + coupling.T)
    diagonal = jax.random.uniform(key_diag, (panel_width,), jnp.float32, 2.0, 4.0)
    identity = jnp.eye(panel_width, dtype=jnp.float32)
    dominant = symmetric * (1.0 - identity) + diagonal[None, :] * identity
    row_numbers = jnp.arange(total_rows)[:, None]
    col_numbers = jnp.arange(total_cols)[None, :]
    base = jnp.where((col_numbers < panel_width) & (row_numbers >= panel_width), 0.5 * base, base)
    full = base.at[:panel_width, :panel_width].set(dominant)
    full = full.reshape(RB, N_ROW, BLK, total_cols).transpose(1, 0, 2, 3).reshape(total_rows, total_cols)
    full = full.T.reshape(CB, N_COL, BLK, total_rows).transpose(1, 0, 2, 3).reshape(total_cols, total_rows).T
    return full


def draw_pattern(key, part):
    key = jax.random.fold_in(key, 11)
    key_second, key_first = jax.random.split(key, 2)
    second_panel = (jax.random.randint(key_second, (NR,), 0, 5) < 3).astype(jnp.int32)
    first_panel = (jax.random.randint(key_first, (NR,), 0, 5) < 3).astype(jnp.int32) * second_panel
    leading = (jnp.arange(NR) < 2 * PB).astype(jnp.int32)
    second_panel = jnp.maximum(second_panel, leading)
    first_panel = jnp.maximum(first_panel, leading)
    return jnp.stack([first_panel, second_panel])


def setup_inputs(seed: int = 0) -> dict:
    keys = jax.random.split(jax.random.key(seed), 3)
    matrix = draw_matrix(jax.random.fold_in(keys[2], 71), 0)
    pattern = draw_pattern(jax.random.fold_in(keys[2], 71), 0)
    return {"matrix": matrix, "pattern": pattern}


precise = lax.Precision.HIGHEST

def storage_to_global(values, groups):
    block_count = values.shape[0] // (groups * BLK)
    return values.reshape(groups, block_count, BLK, values.shape[1]).transpose(1, 0, 2, 3).reshape(values.shape)

def global_to_storage(values, groups):
    block_count = values.shape[0] // (groups * BLK)
    return values.reshape(block_count, groups, BLK, values.shape[1]).transpose(1, 0, 2, 3).reshape(values.shape)

def factor_diag(diagonal_block, half_width):
    identity = jnp.eye(half_width, dtype=jnp.float32)
    leading = jnp.linalg.cholesky(diagonal_block[:half_width, :half_width])
    leading_inv = jax.scipy.linalg.solve_triangular(leading, identity, lower=True)
    lower_left = jnp.dot(diagonal_block[half_width:, :half_width], leading_inv.T, precision=precise)
    reduced = diagonal_block[half_width:, half_width:] - jnp.dot(lower_left, lower_left.T, precision=precise)
    second = jnp.linalg.cholesky(reduced)
    second_inv = jax.scipy.linalg.solve_triangular(second, identity, lower=True)
    corner = -jnp.dot(second_inv, jnp.dot(lower_left, leading_inv, precision=precise), precision=precise)
    zero_block = jnp.zeros((half_width, half_width), jnp.float32)
    factor = jnp.block([[leading, zero_block], [lower_left, second]])
    inverse = jnp.block([[leading_inv, zero_block], [corner, second_inv]])
    return (factor, inverse)

def reference(matrix, pattern):
    panel_width = 2 * PB * BLK
    half_width = PB * BLK
    global_rows = storage_to_global(matrix, N_ROW)
    global_matrix = storage_to_global(global_rows.T, N_COL).T
    factor, inverse = factor_diag(global_matrix[:panel_width, :panel_width], half_width)
    first_mask = jnp.repeat(pattern[0], BLK).astype(jnp.float32)
    second_mask = jnp.repeat(pattern[1], BLK).astype(jnp.float32)
    columns = global_matrix[:, :panel_width]
    masked = jnp.concatenate([columns[:, :half_width] * first_mask[:, None], columns[:, half_width:] * second_mask[:, None]], axis=1)
    solved = jnp.dot(masked, inverse.T, precision=precise)
    row_numbers = jnp.arange(NR * BLK)
    padded_factor = jnp.zeros_like(solved).at[:panel_width].set(factor)
    panel = jnp.where((row_numbers < panel_width)[:, None], padded_factor, solved)
    update = jnp.dot(panel, panel[:NC * BLK].T, precision=precise)
    col_numbers = jnp.arange(NC * BLK)
    keep_mask = (row_numbers >= panel_width)[:, None] & (col_numbers >= panel_width)[None, :]
    schur = jnp.where(keep_mask, global_matrix - update, jnp.zeros_like(update))
    panel_out = global_to_storage(panel, N_ROW)
    schur_out = global_to_storage(global_to_storage(schur, N_ROW).T, N_COL).T
    return (panel_out, schur_out)
```

```python
import jax
import jax.numpy as jnp
from jax import lax
from jax.experimental import pallas as pl
from jax.experimental.pallas import tpu as pltpu
from jax.sharding import PartitionSpec as P

BLK = 128
PB = 4
NB = 2 * PB
PW = NB * BLK
SUB = 16

precise = lax.Precision.HIGHEST
fast = lax.Precision.HIGH


def dot_nn(a, b):
    return jnp.dot(a, b, precision=precise, preferred_element_type=jnp.float32)


def dot_nt(a, b):
    return lax.dot_general(
        a, b, (((1,), (1,)), ((), ())), precision=precise, preferred_element_type=jnp.float32
    )


def lane_copy(x, lane):
    return jnp.broadcast_to(x[:, lane : lane + 1], (8, BLK))


def row_copy(x, row):
    return jnp.broadcast_to(x[row : row + 1, :], (8, BLK))


def reciprocal(x):
    guess = pl.reciprocal(x, approx=True)
    return guess * (2.0 - x * guess)


def invert_base(tiles):
    sub = lax.broadcasted_iota(jnp.int32, (8, BLK), 0)
    lane = lax.broadcasted_iota(jnp.int32, (8, BLK), 1)
    tiles = list(tiles)
    groups = SUB // 8
    result = [None] * 16
    for panel in range(BLK // SUB):
        c0 = panel * SUB
        g0 = panel * groups
        inside = (lane >= c0) & (lane < c0 + SUB)
        cols = [[lane_copy(tiles[g0 + g], c0 + k) for g in range(groups)] for k in range(SUB)]
        rows = [
            jnp.where(inside, jnp.where(lane == sub + (c0 + 8 * g), 1.0, 0.0), tiles[g0 + g])
            for g in range(groups)
        ]
        upper = list(rows)
        pivots = [jnp.ones((8, BLK), jnp.float32)] * groups
        below = {
            (g, k): lane_copy(tiles[g], c0 + k) for g in range(g0 + groups, 16) for k in range(SUB)
        }
        for p in range(SUB):
            gp, sp = p // 8, p % 8
            here = sub == sp
            pivot = row_copy(cols[p][gp], sp)
            inv = reciprocal(pivot)
            pivots[gp] = jnp.where(here, pivot, pivots[gp])
            upper[gp] = jnp.where(here, rows[gp], upper[gp])
            for k in range(p + 1, SUB):
                scaled = row_copy(cols[k][gp], sp) * inv
                for g in range(groups):
                    new = cols[k][g] - cols[p][g] * scaled
                    cols[k][g] = jnp.where(here, scaled, new) if g == gp else new
            scaled = row_copy(rows[gp], sp) * inv
            for g in range(groups):
                new = rows[g] - cols[p][g] * scaled
                rows[g] = jnp.where(here, scaled, new) if g == gp else new
        for g in range(groups):
            result[g0 + g] = jnp.where(
                lane <= sub + (c0 + 8 * g), upper[g] * lax.rsqrt(pivots[g]), 0.0
            )
        if g0 + groups < 16:
            solved = [row_copy(rows[k // 8], k % 8) for k in range(SUB)]
            for g in range(g0 + groups, 16):
                tile = jnp.where(inside, 0.0, tiles[g])
                for k in range(SUB):
                    tile = tile - below[g, k] * solved[k]
                tiles[g] = tile
    return result


def factor_kernel(d_ref, f_ref, v_ref, work, base, sweep):
    work[...] = d_ref[...]
    f_ref[...] = jnp.zeros_like(f_ref)
    lane = lax.broadcasted_iota(jnp.int32, (BLK, PW), 1)
    lower = lax.broadcasted_iota(jnp.int32, (BLK, BLK), 1) <= lax.broadcasted_iota(
        jnp.int32, (BLK, BLK), 0
    )

    def step(k, carry):
        here = pl.ds(pl.multiple_of(k * BLK, BLK), BLK)
        tiles = invert_base([work[k, 8 * g : 8 * g + 8, here] for g in range(16)])
        for g in range(16):
            base[8 * g : 8 * g + 8, :] = tiles[g]
        inv = base[...]
        f_ref[k, :, here] = jnp.where(lower, dot_nt(work[k, :, here], inv), 0.0)
        sweep[...] = dot_nn(inv, work[k])
        sweep[:, here] = inv
        v_ref[k] = jnp.where(lane < (k + 1) * BLK, sweep[...], 0.0)

        def row(i, inner):
            below = dot_nt(work[i, :, here], inv)
            f_ref[i, :, here] = below
            work[i, :, here] = jnp.zeros((BLK, BLK), jnp.float32)
            work[i] = work[i] - dot_nn(below, sweep[...])
            return inner

        lax.fori_loop(k + 1, NB, row, 0)
        return carry

    lax.fori_loop(0, NB, step, 0)


def factor_diag(diagonal):
    shape = (NB, BLK, PW)
    factor, inverse = pl.pallas_call(
        factor_kernel,
        out_shape=[jax.ShapeDtypeStruct(shape, jnp.float32)] * 2,
        scratch_shapes=[
            pltpu.VMEM(shape, jnp.float32),
            pltpu.VMEM((BLK, BLK), jnp.float32),
            pltpu.VMEM((BLK, PW), jnp.float32),
        ],
        compiler_params=pltpu.CompilerParams(vmem_limit_bytes=48 * 2**20),
        cost_estimate=pl.CostEstimate(
            flops=70 * 10**9, bytes_accessed=200 * 10**6, transcendentals=0
        ),
    )(diagonal)
    return factor, inverse.reshape(PW, PW)


def on_device(matrix, pattern):
    rows = lax.axis_size("row")
    cols = lax.axis_size("col")
    row = lax.axis_index("row")
    col = lax.axis_index("col")
    half = PB * BLK
    local_rows = matrix.shape[0]
    row_blocks = local_rows // BLK
    col_blocks = matrix.shape[1] // BLK
    both = ("row", "col")

    def at(r, c):
        return r * cols + c

    same_core = [list(range(0, cols, 2)), list(range(1, cols, 2))]
    corner = lax.all_gather(matrix[:BLK, :BLK], "col", axis=0, axis_index_groups=same_core)
    corner = corner[: NB // 2]
    spread = lax.all_to_all(
        jnp.broadcast_to(corner[None], (rows,) + corner.shape), "row", 0, 0
    )[:NB]
    other = lax.ppermute(
        spread, both, [(at(r, c), at(r, c ^ 1)) for r in range(rows) for c in range(cols)]
    )
    odd = col % 2 == 1
    even_blocks = jnp.where(odd, other, spread)
    odd_blocks = jnp.where(odd, spread, other)
    diagonal = jnp.stack([even_blocks, odd_blocks], axis=2).reshape(NB, NB, BLK, BLK)
    diagonal = diagonal.transpose(0, 2, 1, 3).reshape(NB, BLK, PW)

    mid = local_rows // 2
    moved = lax.ppermute(
        matrix[mid:, :BLK], both, [(at(r, c), at(r, c + NB)) for r in range(rows) for c in range(NB)]
    )
    part = jnp.where(col < NB, matrix[:mid, :BLK], moved)
    panel_cols = lax.all_gather(part, "col", axis=0)

    pattern_grid = pattern.reshape(2, row_blocks, rows)
    own = lax.dynamic_index_in_dim(pattern_grid, row, axis=2, keepdims=False).astype(jnp.float32)
    masks = jnp.repeat(own, BLK, axis=1)

    def natural(x):
        return x.transpose(1, 0, 2).reshape(x.shape[1], PW)

    masked = jnp.concatenate([natural(panel_cols[:NB]), natural(panel_cols[NB:])], axis=0)
    masked = jnp.concatenate(
        [masked[:, :half] * masks[0][:, None], masked[:, half:] * masks[1][:, None]], axis=1
    )

    span = col_blocks * BLK
    share = span // rows
    own_share = lax.dynamic_slice_in_dim(masked, col * share, share, axis=0)
    got_share = lax.ppermute(
        own_share, both, [(at(r, c), at(c, r)) for r in range(rows) for c in range(cols)]
    )
    partner_masked = lax.all_gather(got_share, "row", axis=0, tiled=True)

    factor, inverse = factor_diag(diagonal)
    solved = jnp.einsum("rk,wk->rw", masked, inverse, precision=fast)
    factor_rows = lax.dynamic_index_in_dim(factor, jnp.minimum(row, NB - 1), axis=0, keepdims=False)
    top = jnp.where(row < NB, factor_rows, solved[:BLK])
    panel = jnp.concatenate([top, solved[BLK:]], axis=0)
    partner = jnp.einsum("rk,wk->rw", partner_masked, inverse, precision=fast)
    update = jnp.einsum("rw,cw->rc", panel, partner, precision=fast)
    row_ids = jnp.arange(row_blocks, dtype=jnp.int32) * rows + row
    col_ids = jnp.arange(col_blocks, dtype=jnp.int32) * cols + col
    keep = jnp.repeat(row_ids >= NB, BLK)[:, None] & jnp.repeat(col_ids >= NB, BLK)[None, :]
    schur = jnp.where(keep, matrix - update, jnp.zeros_like(update))
    return (panel, schur)


def solution(mesh):
    in_specs = (P("row", "col"), P())
    out_specs = (P("row", None), P("row", "col"))
    return jax.shard_map(
        on_device, mesh=mesh, in_specs=in_specs, out_specs=out_specs, check_vma=False
    )
```

```python
import jax
import jax.numpy as jnp
import numpy as np
from jax import lax
from jax.experimental import pallas as pl
from jax.experimental.pallas import tpu as pltpu
from jax.sharding import PartitionSpec as P

BLK = 128
PB = 4
NB = 2 * PB
PW = NB * BLK
SUB = 16
SLOTS = 3
HOLD = [
    [[0, 2, 4], [1]],
    [[2, 6], [1, 3, 7]],
    [[2, 4, 6], [3, 5]],
    [[0, 4, 6], [3, 5]],
    [[4, 6], [1, 7]],
    [[0, 4], [1, 5]],
    [[0, 6], [5, 7]],
    [[0, 2], [3, 5, 7]],
]

precise = lax.Precision.HIGHEST


def dot_nn(a, b):
    return jnp.dot(a, b, precision=precise, preferred_element_type=jnp.float32)


def dot_nt(a, b):
    return lax.dot_general(
        a, b, (((1,), (1,)), ((), ())), precision=precise, preferred_element_type=jnp.float32
    )


def lane_copy(x, lane):
    return jnp.broadcast_to(x[:, lane : lane + 1], (8, BLK))


def row_copy(x, row):
    return jnp.broadcast_to(x[row : row + 1, :], (8, BLK))


def reciprocal(x):
    guess = pl.reciprocal(x, approx=True)
    return guess * (2.0 - x * guess)


def invert_base(tiles):
    sub = lax.broadcasted_iota(jnp.int32, (8, BLK), 0)
    lane = lax.broadcasted_iota(jnp.int32, (8, BLK), 1)
    tiles = list(tiles)
    groups = SUB // 8
    result = [None] * 16
    for panel in range(BLK // SUB):
        c0 = panel * SUB
        g0 = panel * groups
        inside = (lane >= c0) & (lane < c0 + SUB)
        cols = [[lane_copy(tiles[g0 + g], c0 + k) for g in range(groups)] for k in range(SUB)]
        rows = [
            jnp.where(inside, jnp.where(lane == sub + (c0 + 8 * g), 1.0, 0.0), tiles[g0 + g])
            for g in range(groups)
        ]
        upper = list(rows)
        pivots = [jnp.ones((8, BLK), jnp.float32)] * groups
        below = {
            (g, k): lane_copy(tiles[g], c0 + k) for g in range(g0 + groups, 16) for k in range(SUB)
        }
        for p in range(SUB):
            gp, sp = p // 8, p % 8
            here = sub == sp
            pivot = row_copy(cols[p][gp], sp)
            inv = reciprocal(pivot)
            pivots[gp] = jnp.where(here, pivot, pivots[gp])
            upper[gp] = jnp.where(here, rows[gp], upper[gp])
            for k in range(p + 1, SUB):
                scaled = row_copy(cols[k][gp], sp) * inv
                for g in range(groups):
                    new = cols[k][g] - cols[p][g] * scaled
                    cols[k][g] = jnp.where(here, scaled, new) if g == gp else new
            scaled = row_copy(rows[gp], sp) * inv
            for g in range(groups):
                new = rows[g] - cols[p][g] * scaled
                rows[g] = jnp.where(here, scaled, new) if g == gp else new
        for g in range(groups):
            result[g0 + g] = jnp.where(
                lane <= sub + (c0 + 8 * g), upper[g] * lax.rsqrt(pivots[g]), 0.0
            )
        if g0 + groups < 16:
            solved = [row_copy(rows[k // 8], k % 8) for k in range(SUB)]
            for g in range(g0 + groups, 16):
                tile = jnp.where(inside, 0.0, tiles[g])
                for k in range(SUB):
                    tile = tile - below[g, k] * solved[k]
                tiles[g] = tile
    return result


def split(x):
    high = x.astype(jnp.bfloat16)
    return high, (x - high.astype(jnp.float32)).astype(jnp.bfloat16)


def factor_kernel(odd_ref, own_ref, other_ref, f_ref, high_ref, low_ref, work, base, sweep):
    odd = odd_ref[0] == 1
    for i in range(NB):
        for parity in range(2):
            for slot, j in enumerate(HOLD[i][parity]):
                mine, theirs = own_ref[i, slot], other_ref[i, slot]
                block = jnp.where(odd, mine, theirs) if parity else jnp.where(odd, theirs, mine)
                work[i, :, j * BLK : (j + 1) * BLK] = block
                if i != j:
                    work[j, :, i * BLK : (i + 1) * BLK] = block.T
    f_ref[...] = jnp.zeros_like(f_ref)
    lane = lax.broadcasted_iota(jnp.int32, (BLK, PW), 1)
    lower = lax.broadcasted_iota(jnp.int32, (BLK, BLK), 1) <= lax.broadcasted_iota(
        jnp.int32, (BLK, BLK), 0
    )

    def step(k, carry):
        here = pl.ds(pl.multiple_of(k * BLK, BLK), BLK)
        tiles = invert_base([work[k, 8 * g : 8 * g + 8, here] for g in range(16)])
        for g in range(16):
            base[8 * g : 8 * g + 8, :] = tiles[g]
        inv = base[...]
        f_ref[k, :, here] = jnp.where(lower, dot_nt(work[k, :, here], inv), 0.0)
        sweep[...] = dot_nn(inv, work[k])
        sweep[:, here] = inv
        high, low = split(jnp.where(lane < (k + 1) * BLK, sweep[...], 0.0))
        high_ref[k] = high
        low_ref[k] = low

        def row(i, inner):
            below = dot_nt(work[i, :, here], inv)
            f_ref[i, :, here] = below
            work[i, :, here] = jnp.zeros((BLK, BLK), jnp.float32)
            work[i] = work[i] - dot_nn(below, sweep[...])
            return inner

        lax.fori_loop(k + 1, NB, row, 0)
        return carry

    lax.fori_loop(0, NB, step, 0)


def factor_diag(odd, own, other):
    shape = (NB, BLK, PW)
    vmem = pl.BlockSpec(memory_space=pltpu.VMEM)
    return pl.pallas_call(
        factor_kernel,
        out_shape=[
            jax.ShapeDtypeStruct(shape, jnp.float32),
            jax.ShapeDtypeStruct(shape, jnp.bfloat16),
            jax.ShapeDtypeStruct(shape, jnp.bfloat16),
        ],
        in_specs=[pl.BlockSpec(memory_space=pltpu.SMEM), vmem, vmem],
        out_specs=[vmem, vmem, vmem],
        scratch_shapes=[
            pltpu.VMEM(shape, jnp.float32),
            pltpu.VMEM((BLK, BLK), jnp.float32),
            pltpu.VMEM((BLK, PW), jnp.float32),
        ],
        compiler_params=pltpu.CompilerParams(vmem_limit_bytes=48 * 2**20),
        cost_estimate=pl.CostEstimate(
            flops=70 * 10**9, bytes_accessed=200 * 10**6, transcendentals=0
        ),
    )(odd, own, other)


def dot3(a, b):
    def term(x, y):
        return lax.dot_general(x, y, (((1,), (1,)), ((), ())), preferred_element_type=jnp.float32)

    return term(a[0], b[0]) + (term(a[0], b[1]) + term(a[1], b[0]))


TILE = 256
STEP = 256


def tail_kernel(
    at_ref,
    pattern_ref,
    w_ref,
    wq_ref,
    m_ref,
    f_ref,
    vh_ref,
    vl_ref,
    p_ref,
    s_ref,
    ah,
    al,
    ph,
    pw,
    qh,
    ql,
):
    tile = pl.program_id(0)
    row, col = at_ref[0], at_ref[1]
    per = TILE // BLK

    def masked(j, first_block, owner, get):
        for b in range(per):
            entry = pattern_ref[j // PB, (first_block + b) * 16 + owner].astype(jnp.float32)
            high, low = split(get(j, b) * entry)
            ah[b * BLK : (b + 1) * BLK, j * BLK : (j + 1) * BLK] = high
            al[b * BLK : (b + 1) * BLK, j * BLK : (j + 1) * BLK] = low

    def solve(store):
        for n in range(PW // STEP):
            rows = slice(n * STEP, (n + 1) * STEP)
            depth = slice(0, (n + 1) * STEP)
            store(
                rows,
                dot3((ah[:, depth], al[:, depth]), (vh_ref[rows, depth], vl_ref[rows, depth])),
            )

    @pl.when(tile == 0)
    def _():
        for h in range(2):
            for j in range(NB):
                masked(
                    j, per * h, col, lambda j, b: wq_ref[2 * j + h, b * BLK : (b + 1) * BLK, :]
                )

            def keep(cols, value):
                high, low = split(value)
                qh[h * TILE : (h + 1) * TILE, cols] = high
                ql[h * TILE : (h + 1) * TILE, cols] = low

            solve(keep)

    for j in range(NB):
        masked(j, per * tile, row, lambda j, b: w_ref[j, b * BLK : (b + 1) * BLK, :])

    def put(cols, value):
        p_ref[:, cols] = value

    solve(put)

    top = (tile == 0) & (row < NB)

    @pl.when(top)
    def _():
        p_ref[:BLK, :] = f_ref[0]

    high, low = split(p_ref[...])
    ph[...] = high
    pw[...] = low
    update = dot3((ph[...], pw[...]), (qh[...], ql[...]))
    s_ref[...] = m_ref[...] - update

    @pl.when(col < NB)
    def _():
        s_ref[:, :BLK] = jnp.zeros((TILE, BLK), jnp.float32)

    @pl.when(top)
    def _():
        s_ref[:BLK, :] = jnp.zeros((BLK, s_ref.shape[1]), jnp.float32)


def tail(at, pattern, panel_cols, partner_cols, matrix, factor, high, low):
    rows, width = matrix.shape
    whole = lambda *_: (0, 0)
    grid_spec = pltpu.PrefetchScalarGridSpec(
        num_scalar_prefetch=2,
        grid=(rows // TILE,),
        in_specs=[
            pl.BlockSpec((NB, TILE, BLK), lambda t, *_: (0, t, 0)),
            pl.BlockSpec((2 * NB, TILE, BLK), lambda t, *_: (0, 0, 0)),
            pl.BlockSpec((TILE, width), lambda t, *_: (t, 0)),
            pl.BlockSpec((1, BLK, PW), lambda t, at, _: (jnp.minimum(at[0], NB - 1), 0, 0)),
            pl.BlockSpec((PW, PW), whole),
            pl.BlockSpec((PW, PW), whole),
        ],
        out_specs=[
            pl.BlockSpec((TILE, PW), lambda t, *_: (t, 0)),
            pl.BlockSpec((TILE, width), lambda t, *_: (t, 0)),
        ],
        scratch_shapes=[
            pltpu.VMEM((TILE, PW), jnp.bfloat16),
            pltpu.VMEM((TILE, PW), jnp.bfloat16),
            pltpu.VMEM((TILE, PW), jnp.bfloat16),
            pltpu.VMEM((TILE, PW), jnp.bfloat16),
            pltpu.VMEM((width, PW), jnp.bfloat16),
            pltpu.VMEM((width, PW), jnp.bfloat16),
        ],
    )
    return pl.pallas_call(
        tail_kernel,
        grid_spec=grid_spec,
        out_shape=[
            jax.ShapeDtypeStruct((rows, PW), jnp.float32),
            jax.ShapeDtypeStruct((rows, width), jnp.float32),
        ],
        compiler_params=pltpu.CompilerParams(vmem_limit_bytes=48 * 2**20),
        cost_estimate=pl.CostEstimate(
            flops=10 * 10**9, bytes_accessed=20 * 10**6, transcendentals=0
        ),
    )(at, pattern, panel_cols, partner_cols, matrix, factor, high, low)


def on_device(matrix, pattern):
    rows = lax.axis_size("row")
    cols = lax.axis_size("col")
    row = lax.axis_index("row")
    col = lax.axis_index("col")
    both = ("row", "col")

    def at(r, c):
        return r * cols + c

    def pairs(target, width=cols):
        return [(at(r, c), at(*target(r, c))) for r in range(rows) for c in range(width)]

    first = matrix[:, :BLK]
    panel_cols = lax.all_gather(first, "col", axis=0)

    same_core = [list(range(0, cols, 2)), list(range(1, cols, 2))]
    corner = jnp.broadcast_to(first[:BLK][None], (cols // 2, BLK, BLK))
    corner = lax.all_to_all(corner, "col", 0, 0, axis_index_groups=same_core)
    table = np.zeros((NB, 2, SLOTS), np.int32)
    for i in range(NB):
        for parity in range(2):
            for slot, j in enumerate(HOLD[i][parity]):
                table[i, parity, slot] = j // 2
    chosen = jnp.asarray(table)[jnp.minimum(row, NB - 1), col % 2]
    corner = jnp.stack(
        [lax.dynamic_index_in_dim(corner, chosen[s], axis=0, keepdims=False) for s in range(SLOTS)]
    )
    own = lax.all_to_all(jnp.broadcast_to(corner[None], (rows,) + corner.shape), "row", 0, 0)
    own = own[:NB]
    other = lax.ppermute(own, both, pairs(lambda r, c: (r, c ^ 1)))

    span = matrix.shape[1] // 2
    shares = [
        lax.ppermute(
            first[h * span : (h + 1) * span], both, pairs(lambda r, c, h=h: (2 * c + h, r), NB)
        )
        for h in range(2)
    ]
    share = jnp.where(row % 2 == 0, shares[0], shares[1])
    partner_cols = lax.all_gather(share, "row", axis=0)

    factor, high, low = factor_diag((col % 2).astype(jnp.int32).reshape(1), own, other)
    place = jnp.stack([row, col]).astype(jnp.int32)
    panel, schur = tail(
        place,
        pattern,
        panel_cols,
        partner_cols,
        matrix,
        factor,
        high.reshape(PW, PW),
        low.reshape(PW, PW),
    )
    return (panel, schur)


def solution(mesh):
    in_specs = (P("row", "col"), P())
    out_specs = (P("row", None), P("row", "col"))
    return jax.shard_map(
        on_device, mesh=mesh, in_specs=in_specs, out_specs=out_specs, check_vma=False
    )
```

```python
import jax
import jax.numpy as jnp
from jax import lax
from jax.experimental import pallas as pl
from jax.experimental.pallas import tpu as pltpu
from jax.sharding import PartitionSpec as P

BLK = 128
PB = 4
NB = 2 * PB
PW = NB * BLK
SUB = 16
SLOTS = 3
HOLD = [
    [[0, 2, 4], [1]],
    [[2, 6], [1, 3, 7]],
    [[2, 4, 6], [3, 5]],
    [[0, 4, 6], [3, 5]],
    [[4, 6], [1, 7]],
    [[0, 4], [1, 5]],
    [[0, 6], [5, 7]],
    [[0, 2], [3, 5, 7]],
]


def split(x):
    high = x.astype(jnp.bfloat16)
    return high, (x - high.astype(jnp.float32)).astype(jnp.bfloat16)


def split3(x):
    high = x.astype(jnp.bfloat16)
    rest = x - high.astype(jnp.float32)
    mid = rest.astype(jnp.bfloat16)
    return high, mid, (rest - mid.astype(jnp.float32)).astype(jnp.bfloat16)


def left6(x):
    high, mid, low = split3(x)
    return jnp.concatenate([high, mid, high, mid, high, low], axis=1)


def right6(x, axis):
    high, mid, low = split3(x)
    return jnp.concatenate([high, high, mid, mid, low, high], axis=axis)


def dot_nn(a, b):
    return jnp.dot(a, b, preferred_element_type=jnp.float32)


def dot_nt(a, b):
    return lax.dot_general(a, b, (((1,), (1,)), ((), ())), preferred_element_type=jnp.float32)


def lane_copy(x, lane):
    return jnp.broadcast_to(x[:, lane : lane + 1], (8, BLK))


def row_copy(x, row):
    return jnp.broadcast_to(x[row : row + 1, :], (8, BLK))


def reciprocal(x):
    return pl.reciprocal(x, approx=True)


def invert_base(tiles):
    sub = lax.broadcasted_iota(jnp.int32, (8, BLK), 0)
    lane = lax.broadcasted_iota(jnp.int32, (8, BLK), 1)
    tiles = list(tiles)
    result = []
    for panel in range(BLK // 8):
        c0 = panel * 8
        inside = (lane >= c0) & (lane < c0 + 8)
        cols = [lane_copy(tiles[panel], c0 + k) for k in range(8)]
        rows = jnp.where(inside, jnp.where(lane == sub + c0, 1.0, 0.0), tiles[panel])
        upper = rows
        pivots = jnp.ones((8, BLK), jnp.float32)
        below = {(g, k): lane_copy(tiles[g], c0 + k) for g in range(panel + 1, 16) for k in range(8)}
        for p in range(0, 8, 2):
            one, two = sub == p, sub == p + 1
            pair = one | two
            a, b = row_copy(cols[p], p), row_copy(cols[p + 1], p)
            c = row_copy(cols[p + 1], p + 1)
            det = a * c - b * b
            inv_det, inv_a = reciprocal(det), reciprocal(a)
            aa, ab, bb = c * inv_det, b * inv_det, a * inv_det
            top, low = row_copy(rows, p), row_copy(rows, p + 1)
            pivots = jnp.where(one, a, jnp.where(two, det * inv_a, pivots))
            upper = jnp.where(one, top, jnp.where(two, low - b * inv_a * top, upper))

            def swept(x, y, target):
                u, v = aa * x - ab * y, bb * y - ab * x
                return jnp.where(pair, jnp.where(one, u, v), target - (cols[p] * u + cols[p + 1] * v))

            for k in range(p + 2, 8):
                cols[k] = swept(row_copy(cols[k], p), row_copy(cols[k], p + 1), cols[k])
            rows = swept(top, low, rows)
        result.append(jnp.where(lane <= sub + c0, upper * lax.rsqrt(pivots), 0.0))
        if panel < 15:
            solved = [row_copy(rows, k) for k in range(8)]
            for g in range(panel + 1, 16):
                parts = [below[g, k] * solved[k] for k in range(8)]
                while len(parts) > 1:
                    parts = [parts[m] + parts[m + 1] for m in range(0, len(parts), 2)]
                tiles[g] = jnp.where(inside, 0.0, tiles[g]) - parts[0]
    return result


def invert_into(base, block):
    for g, tile in enumerate(invert_base([block[8 * g : 8 * g + 8, :] for g in range(16)])):
        base[8 * g : 8 * g + 8, :] = tile


def lower_part(x):
    shape = (BLK, BLK)
    keep = lax.broadcasted_iota(jnp.int32, shape, 1) <= lax.broadcasted_iota(jnp.int32, shape, 0)
    return jnp.where(keep, x, 0.0)


def factor_steps(first, last, work, diag, head, base):
    def step(k, carry):
        here = pl.ds(pl.multiple_of(k * BLK, BLK), BLK)
        there = pl.ds(pl.multiple_of(k * BLK + BLK, BLK), BLK)
        inv, block = base[...], head[...]
        inv_left, inv_right = left6(inv), right6(inv, 1)
        below = dot_nt(left6(work[k + 1, :, here]), inv_right)
        beside = dot_nn(inv_left, right6(work[k, :, there], 0))
        following = work[k + 1, :, there] - dot_nn(left6(below), right6(beside, 0))
        head[...] = following
        tiles = invert_base([following[8 * g : 8 * g + 8, :] for g in range(16)])
        diag[k] = lower_part(dot_nt(left6(block), inv_right))
        work[k] = dot_nn(inv_left, right6(work[k], 0))
        work[k, :, here] = inv
        sweep = right6(work[k], 0)
        for i in range(1, NB):
            block = work[i, :, here]
            below = left6(jnp.where(i > k, dot_nt(left6(block), inv_right), 0.0))
            work[i, :, here] = jnp.where(i > k, 0.0, block)
            work[i] = work[i] - dot_nn(below, sweep)
        for g in range(16):
            base[8 * g : 8 * g + 8, :] = tiles[g]
        return carry

    lax.fori_loop(first, last, step, 0)


FIRST_STEPS = 3


def start_kernel(odd_ref, own_ref, other_ref, work, diag, head, base):
    odd = odd_ref[0] == 1
    for i in range(NB):
        for parity in range(2):
            for slot, j in enumerate(HOLD[i][parity]):
                parts = []
                for at in (i, i + NB):
                    mine, theirs = own_ref[at, slot], other_ref[at, slot]
                    parts.append(jnp.where(odd == (parity == 1), mine, theirs))
                block = jnp.concatenate(parts, axis=0)
                work[i, :, j * BLK : (j + 1) * BLK] = block
                if i != j:
                    work[j, :, i * BLK : (i + 1) * BLK] = block.T
    head[...] = work[0, :, :BLK]
    invert_into(base, head)
    factor_steps(0, FIRST_STEPS, work, diag, head, base)


def finish_kernel(w_in, d_in, h_in, b_in, work, diag, head, base):
    factor_steps(FIRST_STEPS, NB - 1, work, diag, head, base)
    last = NB - 1
    inv = base[...]
    diag[last] = lower_part(dot_nt(left6(head[...]), right6(inv, 1)))
    work[last] = dot_nn(left6(inv), right6(work[last], 0))
    work[last, :, last * BLK :] = inv


STATE = [
    jax.ShapeDtypeStruct((NB, BLK, PW), jnp.float32),
    jax.ShapeDtypeStruct((NB, BLK, BLK), jnp.float32),
    jax.ShapeDtypeStruct((BLK, BLK), jnp.float32),
    jax.ShapeDtypeStruct((BLK, BLK), jnp.float32),
]


def factor_call(kernel, scalars, operands, aliases, share):
    vmem = pl.BlockSpec(memory_space=pltpu.VMEM)
    return pl.pallas_call(
        kernel,
        out_shape=STATE,
        in_specs=[pl.BlockSpec(memory_space=pltpu.SMEM)] * len(scalars) + [vmem] * len(operands),
        out_specs=[vmem] * len(STATE),
        input_output_aliases=aliases,
        compiler_params=pltpu.CompilerParams(vmem_limit_bytes=32 * 2**20),
        cost_estimate=pl.CostEstimate(
            flops=share * 10**10, bytes_accessed=share * 25 * 10**6, transcendentals=0
        ),
    )(*scalars, *operands)


def dot3(a, b):
    def term(x, y):
        return lax.dot_general(x, y, (((1,), (1,)), ((), ())), preferred_element_type=jnp.float32)

    return term(a[0], b[0]) + (term(a[0], b[1]) + term(a[1], b[0]))


TILE = 256
STEP = 256


def tail_kernel(
    at_ref, pattern_ref, w_ref, wq_ref, m_ref, work, diag, p_ref, s_ref, ah, al, qh, ql, vh, vl
):
    tile = pl.program_id(0)
    row, col = at_ref[0], at_ref[1]
    per = TILE // BLK

    def masked(j, first_block, owner, get):
        for b in range(per):
            entry = pattern_ref[j // PB, (first_block + b) * 16 + owner].astype(jnp.float32)
            high, low = split(get(j, b) * entry)
            ah[b * BLK : (b + 1) * BLK, j * BLK : (j + 1) * BLK] = high
            al[b * BLK : (b + 1) * BLK, j * BLK : (j + 1) * BLK] = low

    def solve(store):
        for n in range(PW // STEP):
            rows = slice(n * STEP, (n + 1) * STEP)
            depth = slice(0, (n + 1) * STEP)
            store(rows, dot3((ah[:, depth], al[:, depth]), (vh[rows, depth], vl[rows, depth])))

    @pl.when(tile == 0)
    def _():
        lane = lax.broadcasted_iota(jnp.int32, (BLK, PW), 1)
        for k in range(NB):
            high, low = split(jnp.where(lane < (k + 1) * BLK, work[k], 0.0))
            vh[k * BLK : (k + 1) * BLK, :] = high
            vl[k * BLK : (k + 1) * BLK, :] = low
        for h in range(qh.shape[0] // TILE):
            for j in range(NB):
                masked(
                    j,
                    per * h,
                    col,
                    lambda j, b: wq_ref[(2 * j + h) ^ col, b * BLK : (b + 1) * BLK, :],
                )

            def keep(cols, value):
                high, low = split(value)
                qh[h * TILE : (h + 1) * TILE, cols] = high
                ql[h * TILE : (h + 1) * TILE, cols] = low

            solve(keep)

    for j in range(NB):
        masked(j, per * tile, row, lambda j, b: w_ref[j, b * BLK : (b + 1) * BLK, :])

    def put(cols, value):
        p_ref[:, cols] = value

    solve(put)

    top = (tile == 0) & (row < NB)

    @pl.when(top)
    def _():
        here = pl.ds(pl.multiple_of(row * BLK, BLK), BLK)
        for k in range(NB):
            block = jnp.where(k < row, work[k, :, here].T, 0.0)
            p_ref[:BLK, k * BLK : (k + 1) * BLK] = jnp.where(k == row, diag[row], block)

    s_ref[...] = m_ref[...] - dot3(split(p_ref[...]), (qh[...], ql[...]))

    @pl.when(col < NB)
    def _():
        s_ref[:, :BLK] = jnp.zeros((TILE, BLK), jnp.float32)

    @pl.when(top)
    def _():
        s_ref[:BLK, :] = jnp.zeros((BLK, s_ref.shape[1]), jnp.float32)


def tail(at, pattern, panel_cols, partner_cols, matrix, work, diag):
    rows, width = matrix.shape
    pieces = partner_cols.shape
    grid_spec = pltpu.PrefetchScalarGridSpec(
        num_scalar_prefetch=2,
        grid=(rows // TILE,),
        in_specs=[
            pl.BlockSpec((NB, TILE, BLK), lambda t, *_: (0, t, 0)),
            pl.BlockSpec(pieces, lambda t, *_: (0, 0, 0)),
            pl.BlockSpec((TILE, width), lambda t, *_: (t, 0)),
            pl.BlockSpec((NB, BLK, PW), lambda t, *_: (0, 0, 0)),
            pl.BlockSpec((NB, BLK, BLK), lambda t, *_: (0, 0, 0)),
        ],
        out_specs=[
            pl.BlockSpec((TILE, PW), lambda t, *_: (t, 0)),
            pl.BlockSpec((TILE, width), lambda t, *_: (t, 0)),
        ],
        scratch_shapes=[
            pltpu.VMEM((TILE, PW), jnp.bfloat16),
            pltpu.VMEM((TILE, PW), jnp.bfloat16),
            pltpu.VMEM((width, PW), jnp.bfloat16),
            pltpu.VMEM((width, PW), jnp.bfloat16),
            pltpu.VMEM((PW, PW), jnp.bfloat16),
            pltpu.VMEM((PW, PW), jnp.bfloat16),
        ],
    )
    return pl.pallas_call(
        tail_kernel,
        grid_spec=grid_spec,
        out_shape=[
            jax.ShapeDtypeStruct((rows, PW), jnp.float32),
            jax.ShapeDtypeStruct((rows, width), jnp.float32),
        ],
        compiler_params=pltpu.CompilerParams(vmem_limit_bytes=48 * 2**20),
        cost_estimate=pl.CostEstimate(
            flops=10 * 10**9, bytes_accessed=20 * 10**6, transcendentals=0
        ),
    )(at, pattern, panel_cols, partner_cols, matrix, work, diag)


def pack_kernel(at_ref, corner_ref, out_ref):
    row, odd = at_ref[0] % NB, at_ref[1] % 2
    for i in range(NB):
        for parity in range(2):

            @pl.when((row == i) & (odd == parity))
            def _():
                for slot in range(SLOTS):
                    held = HOLD[i][parity]
                    block = corner_ref[held[min(slot, len(held) - 1)] // 2]
                    for target in range(out_ref.shape[0]):
                        out_ref[target, slot] = block


def pack(at, corner, rows):
    return pl.pallas_call(
        pack_kernel,
        out_shape=jax.ShapeDtypeStruct((rows, SLOTS) + corner.shape[1:], jnp.float32),
        in_specs=[
            pl.BlockSpec(memory_space=pltpu.SMEM),
            pl.BlockSpec(memory_space=pltpu.VMEM),
        ],
        out_specs=pl.BlockSpec(memory_space=pltpu.VMEM),
        compiler_params=pltpu.CompilerParams(vmem_limit_bytes=16 * 2**20),
    )(at, corner)


def on_device(matrix, pattern):
    rows = lax.axis_size("row")
    cols = lax.axis_size("col")
    row = lax.axis_index("row")
    col = lax.axis_index("col")
    both = ("row", "col")

    def at(r, c):
        return r * cols + c

    def pairs(target, width=cols):
        return [(at(r, c), at(*target(r, c))) for r in range(rows) for c in range(width)]

    first = matrix[:, :BLK]
    cut = BLK // 2
    groups = [
        [at(r + o, c) for o in (0, NB) for c in range(core, cols, 2)]
        for r in range(NB)
        for core in range(2)
    ]
    corner = jnp.repeat(first[:BLK].reshape(2, cut, BLK), cols // 2, axis=0)
    corner = lax.all_to_all(corner, both, 0, 0, axis_index_groups=groups)
    first, corner = lax.optimization_barrier((first, corner))

    place = jnp.stack([row, col]).astype(jnp.int32)

    panel_cols = lax.all_gather(first, "col", axis=0)

    own = lax.all_to_all(pack(place, corner, rows), "row", 0, 0)
    first, own = lax.optimization_barrier((first, own))
    other = lax.ppermute(own, both, pairs(lambda r, c: (r, c ^ 1)))

    span = matrix.shape[1] // 2
    shares = [
        lax.ppermute(
            first[h * span : (h + 1) * span],
            both,
            pairs(lambda r, c, h=h: ((2 * c + h) ^ r, r), NB),
        )
        for h in range(2)
    ]
    odd = (col % 2).astype(jnp.int32).reshape(1)
    state = factor_call(start_kernel, (odd,), (own, other), {}, 3)
    shares, state = lax.optimization_barrier((shares, state))
    share = jnp.where((row ^ col) % 2 == 0, shares[0], shares[1])
    partner_cols = lax.all_to_all(
        jnp.broadcast_to(share[None], (rows,) + share.shape), "row", 0, 0
    )
    work, diag, _, _ = factor_call(finish_kernel, (), state, {i: i for i in range(4)}, 4)
    panel, schur = tail(place, pattern, panel_cols, partner_cols, matrix, work, diag)
    return (panel, schur)


def solution(mesh):
    in_specs = (P("row", "col"), P())
    out_specs = (P("row", None), P("row", "col"))
    return jax.shard_map(
        on_device, mesh=mesh, in_specs=in_specs, out_specs=out_specs, check_vma=False
    )
```

```python
import jax
import jax.numpy as jnp
from jax import lax
from jax.experimental import pallas as pl
from jax.experimental.pallas import tpu as pltpu
from jax.sharding import PartitionSpec as P

BLK = 128
PB = 4
NB = 2 * PB
PW = NB * BLK
SUB = 16
SLOTS = 3
HOLD = [
    [[0, 2, 4], [1]],
    [[2, 6], [1, 3, 7]],
    [[2, 4, 6], [3, 5]],
    [[0, 4, 6], [3, 5]],
    [[4, 6], [1, 7]],
    [[0, 4], [1, 5]],
    [[0, 6], [5, 7]],
    [[0, 2], [3, 5, 7]],
]


def split(x):
    high = x.astype(jnp.bfloat16)
    return high, (x - high.astype(jnp.float32)).astype(jnp.bfloat16)


def split3(x):
    high = x.astype(jnp.bfloat16)
    rest = x - high.astype(jnp.float32)
    mid = rest.astype(jnp.bfloat16)
    return high, mid, (rest - mid.astype(jnp.float32)).astype(jnp.bfloat16)


def left6(x):
    high, mid, low = split3(x)
    return jnp.concatenate([high, mid, high, mid, high, low], axis=1)


def right6(x, axis):
    high, mid, low = split3(x)
    return jnp.concatenate([high, high, mid, mid, low, high], axis=axis)


def dot_nn(a, b):
    return jnp.dot(a, b, preferred_element_type=jnp.float32)


def dot_nt(a, b):
    return lax.dot_general(a, b, (((1,), (1,)), ((), ())), preferred_element_type=jnp.float32)


def lane_copy(x, lane):
    return jnp.broadcast_to(x[:, lane : lane + 1], (8, BLK))


def row_copy(x, row):
    return jnp.broadcast_to(x[row : row + 1, :], (8, BLK))


def reciprocal(x):
    return pl.reciprocal(x, approx=True)


def invert_base(tiles):
    sub = lax.broadcasted_iota(jnp.int32, (8, BLK), 0)
    lane = lax.broadcasted_iota(jnp.int32, (8, BLK), 1)
    tiles = list(tiles)
    result = []
    for panel in range(BLK // 8):
        c0 = panel * 8
        inside = (lane >= c0) & (lane < c0 + 8)
        cols = [lane_copy(tiles[panel], c0 + k) for k in range(8)]
        rows = jnp.where(inside, jnp.where(lane == sub + c0, 1.0, 0.0), tiles[panel])
        upper = rows
        pivots = jnp.ones((8, BLK), jnp.float32)
        below = {(g, k): lane_copy(tiles[g], c0 + k) for g in range(panel + 1, 16) for k in range(8)}
        for p in range(0, 8, 2):
            one, two = sub == p, sub == p + 1
            pair = one | two
            a, b = row_copy(cols[p], p), row_copy(cols[p + 1], p)
            c = row_copy(cols[p + 1], p + 1)
            det = a * c - b * b
            inv_det, inv_a = reciprocal(det), reciprocal(a)
            aa, ab, bb = c * inv_det, b * inv_det, a * inv_det
            top, low = row_copy(rows, p), row_copy(rows, p + 1)
            pivots = jnp.where(one, a, jnp.where(two, det * inv_a, pivots))
            upper = jnp.where(one, top, jnp.where(two, low - b * inv_a * top, upper))

            def swept(x, y, target):
                u, v = aa * x - ab * y, bb * y - ab * x
                return jnp.where(pair, jnp.where(one, u, v), target - (cols[p] * u + cols[p + 1] * v))

            for k in range(p + 2, 8):
                cols[k] = swept(row_copy(cols[k], p), row_copy(cols[k], p + 1), cols[k])
            rows = swept(top, low, rows)
        result.append(jnp.where(lane <= sub + c0, upper * lax.rsqrt(pivots), 0.0))
        if panel < 15:
            solved = [row_copy(rows, k) for k in range(8)]
            for g in range(panel + 1, 16):
                parts = [below[g, k] * solved[k] for k in range(8)]
                while len(parts) > 1:
                    parts = [parts[m] + parts[m + 1] for m in range(0, len(parts), 2)]
                tiles[g] = jnp.where(inside, 0.0, tiles[g]) - parts[0]
    return result


def invert_into(base, block):
    for g, tile in enumerate(invert_base([block[8 * g : 8 * g + 8, :] for g in range(16)])):
        base[8 * g : 8 * g + 8, :] = tile


def lower_part(x):
    shape = (BLK, BLK)
    keep = lax.broadcasted_iota(jnp.int32, shape, 1) <= lax.broadcasted_iota(jnp.int32, shape, 0)
    return jnp.where(keep, x, 0.0)


def factor_steps(first, last, work, diag, head, base):
    def step(k, carry):
        here = pl.ds(pl.multiple_of(k * BLK, BLK), BLK)
        there = pl.ds(pl.multiple_of(k * BLK + BLK, BLK), BLK)
        inv, block = base[...], head[...]
        inv_left, inv_right = left6(inv), right6(inv, 1)
        below = dot_nt(left6(work[k + 1, :, here]), inv_right)
        beside = dot_nn(inv_left, right6(work[k, :, there], 0))
        following = work[k + 1, :, there] - dot_nn(left6(below), right6(beside, 0))
        head[...] = following
        tiles = invert_base([following[8 * g : 8 * g + 8, :] for g in range(16)])
        diag[k] = lower_part(dot_nt(left6(block), inv_right))
        work[k] = dot_nn(inv_left, right6(work[k], 0))
        work[k, :, here] = inv
        sweep = right6(work[k], 0)
        for i in range(1, NB):
            block = work[i, :, here]
            below = left6(jnp.where(i > k, dot_nt(left6(block), inv_right), 0.0))
            work[i, :, here] = jnp.where(i > k, 0.0, block)
            work[i] = work[i] - dot_nn(below, sweep)
        for g in range(16):
            base[8 * g : 8 * g + 8, :] = tiles[g]
        return carry

    lax.fori_loop(first, last, step, 0)


FIRST_STEPS = 3


def start_kernel(odd_ref, own_ref, other_ref, work, diag, head, base):
    odd = odd_ref[0] == 1
    for i in range(NB):
        for parity in range(2):
            for slot, j in enumerate(HOLD[i][parity]):
                parts = []
                for at in (i, i + NB):
                    mine, theirs = own_ref[at, slot], other_ref[at, slot]
                    parts.append(jnp.where(odd == (parity == 1), mine, theirs))
                block = jnp.concatenate(parts, axis=0)
                work[i, :, j * BLK : (j + 1) * BLK] = block
                if i != j:
                    work[j, :, i * BLK : (i + 1) * BLK] = block.T
    head[...] = work[0, :, :BLK]
    invert_into(base, head)
    factor_steps(0, FIRST_STEPS, work, diag, head, base)


def finish_kernel(w_in, d_in, h_in, b_in, work, diag, head, base):
    factor_steps(FIRST_STEPS, NB - 1, work, diag, head, base)
    last = NB - 1
    inv = base[...]
    diag[last] = lower_part(dot_nt(left6(head[...]), right6(inv, 1)))
    work[last] = dot_nn(left6(inv), right6(work[last], 0))
    work[last, :, last * BLK :] = inv


STATE = [
    jax.ShapeDtypeStruct((NB, BLK, PW), jnp.float32),
    jax.ShapeDtypeStruct((NB, BLK, BLK), jnp.float32),
    jax.ShapeDtypeStruct((BLK, BLK), jnp.float32),
    jax.ShapeDtypeStruct((BLK, BLK), jnp.float32),
]


def factor_call(kernel, scalars, operands, aliases, share):
    vmem = pl.BlockSpec(memory_space=pltpu.VMEM)
    return pl.pallas_call(
        kernel,
        out_shape=STATE,
        in_specs=[pl.BlockSpec(memory_space=pltpu.SMEM)] * len(scalars) + [vmem] * len(operands),
        out_specs=[vmem] * len(STATE),
        input_output_aliases=aliases,
        compiler_params=pltpu.CompilerParams(vmem_limit_bytes=24 * 2**20),
        cost_estimate=pl.CostEstimate(
            flops=share * 10**10, bytes_accessed=share * 25 * 10**6, transcendentals=0
        ),
    )(*scalars, *operands)


def dot3(a, b):
    return dot_nt(
        jnp.concatenate([a[0], a[1], a[0]], axis=1), jnp.concatenate([b[0], b[0], b[1]], axis=1)
    )


TILE = 512
STEP = 256


def tail_kernel(
    at_ref, pattern_ref, w_ref, wq_ref, m_ref, work, diag, p_ref, s_ref, ah, al, qh, ql, vh, vl
):
    tile = pl.program_id(0)
    row, col = at_ref[0], at_ref[1]
    per = TILE // BLK

    def masked(j, first_block, owner, get):
        for b in range(per):
            entry = pattern_ref[j // PB, (first_block + b) * 16 + owner].astype(jnp.float32)
            high, low = split(get(j, b) * entry)
            ah[b * BLK : (b + 1) * BLK, j * BLK : (j + 1) * BLK] = high
            al[b * BLK : (b + 1) * BLK, j * BLK : (j + 1) * BLK] = low

    def solve(store):
        for n in range(PW // STEP):
            rows = slice(n * STEP, (n + 1) * STEP)
            depth = slice(0, (n + 1) * STEP)
            store(rows, dot3((ah[:, depth], al[:, depth]), (vh[rows, depth], vl[rows, depth])))

    @pl.when(tile == 0)
    def _():
        lane = lax.broadcasted_iota(jnp.int32, (BLK, PW), 1)
        for k in range(NB):
            high, low = split(jnp.where(lane < (k + 1) * BLK, work[k], 0.0))
            vh[k * BLK : (k + 1) * BLK, :] = high
            vl[k * BLK : (k + 1) * BLK, :] = low
        for h in range(qh.shape[0] // TILE):
            for j in range(NB):
                masked(
                    j,
                    per * h,
                    col,
                    lambda j, b: wq_ref[
                        (2 * j + (per * h + b) // 2) ^ col, b % 2 * BLK : (b % 2 + 1) * BLK, :
                    ],
                )

            def keep(cols, value):
                high, low = split(value)
                qh[h * TILE : (h + 1) * TILE, cols] = high
                ql[h * TILE : (h + 1) * TILE, cols] = low

            solve(keep)

    for j in range(NB):
        masked(j, per * tile, row, lambda j, b: w_ref[j, b * BLK : (b + 1) * BLK, :])

    def put(cols, value):
        p_ref[:, cols] = value

    solve(put)

    top = (tile == 0) & (row < NB)

    @pl.when(top)
    def _():
        here = pl.ds(pl.multiple_of(row * BLK, BLK), BLK)
        for k in range(NB):
            block = jnp.where(k < row, work[k, :, here].T, 0.0)
            p_ref[:BLK, k * BLK : (k + 1) * BLK] = jnp.where(k == row, diag[row], block)

    s_ref[...] = m_ref[...] - dot3(split(p_ref[...]), (qh[...], ql[...]))

    @pl.when(col < NB)
    def _():
        s_ref[:, :BLK] = jnp.zeros((TILE, BLK), jnp.float32)

    @pl.when(top)
    def _():
        s_ref[:BLK, :] = jnp.zeros((BLK, s_ref.shape[1]), jnp.float32)


def tail(at, pattern, panel_cols, partner_cols, matrix, work, diag):
    rows, width = matrix.shape
    grid_spec = pltpu.PrefetchScalarGridSpec(
        num_scalar_prefetch=2,
        grid=(rows // TILE,),
        in_specs=[
            pl.BlockSpec((NB, TILE, BLK), lambda t, *_: (0, t, 0)),
            pl.BlockSpec(memory_space=pltpu.VMEM),
            pl.BlockSpec((TILE, width), lambda t, *_: (t, 0)),
            pl.BlockSpec(memory_space=pltpu.VMEM),
            pl.BlockSpec(memory_space=pltpu.VMEM),
        ],
        out_specs=[
            pl.BlockSpec((TILE, PW), lambda t, *_: (t, 0)),
            pl.BlockSpec((TILE, width), lambda t, *_: (t, 0)),
        ],
        scratch_shapes=[
            pltpu.VMEM((TILE, PW), jnp.bfloat16),
            pltpu.VMEM((TILE, PW), jnp.bfloat16),
            pltpu.VMEM((width, PW), jnp.bfloat16),
            pltpu.VMEM((width, PW), jnp.bfloat16),
            pltpu.VMEM((PW, PW), jnp.bfloat16),
            pltpu.VMEM((PW, PW), jnp.bfloat16),
        ],
    )
    return pl.pallas_call(
        tail_kernel,
        grid_spec=grid_spec,
        out_shape=[
            jax.ShapeDtypeStruct((rows, PW), jnp.float32),
            jax.ShapeDtypeStruct((rows, width), jnp.float32),
        ],
        compiler_params=pltpu.CompilerParams(vmem_limit_bytes=44 * 2**20),
        cost_estimate=pl.CostEstimate(
            flops=10 * 10**9, bytes_accessed=20 * 10**6, transcendentals=0
        ),
    )(at, pattern, panel_cols, partner_cols, matrix, work, diag)


def pack_kernel(at_ref, corner_ref, out_ref):
    row, odd = at_ref[0] % NB, at_ref[1] % 2
    for i in range(NB):
        for parity in range(2):

            @pl.when((row == i) & (odd == parity))
            def _():
                for slot in range(SLOTS):
                    held = HOLD[i][parity]
                    block = corner_ref[held[min(slot, len(held) - 1)] // 2]
                    for target in range(out_ref.shape[0]):
                        out_ref[target, slot] = block


def pack(at, corner, rows):
    return pl.pallas_call(
        pack_kernel,
        out_shape=jax.ShapeDtypeStruct((rows, SLOTS) + corner.shape[1:], jnp.float32),
        in_specs=[
            pl.BlockSpec(memory_space=pltpu.SMEM),
            pl.BlockSpec(memory_space=pltpu.VMEM),
        ],
        out_specs=pl.BlockSpec(memory_space=pltpu.VMEM),
        compiler_params=pltpu.CompilerParams(vmem_limit_bytes=16 * 2**20),
    )(at, corner)


def on_device(matrix, pattern):
    rows = lax.axis_size("row")
    cols = lax.axis_size("col")
    row = lax.axis_index("row")
    col = lax.axis_index("col")
    both = ("row", "col")

    def at(r, c):
        return r * cols + c

    def pairs(target, width=cols):
        return [(at(r, c), at(*target(r, c))) for r in range(rows) for c in range(width)]

    first = matrix[:, :BLK]
    cut = BLK // 2
    groups = [
        [at(r + o, c) for o in (0, NB) for c in range(core, cols, 2)]
        for r in range(NB)
        for core in range(2)
    ]
    corner = jnp.repeat(first[:BLK].reshape(2, cut, BLK), cols // 2, axis=0)
    corner = lax.all_to_all(corner, both, 0, 0, axis_index_groups=groups)
    first, corner = lax.optimization_barrier((first, corner))

    place = jnp.stack([row, col]).astype(jnp.int32)

    panel_cols = lax.all_gather(first, "col", axis=0)

    own = lax.all_to_all(pack(place, corner, rows), "row", 0, 0)
    first, own = lax.optimization_barrier((first, own))
    other = lax.ppermute(own, both, pairs(lambda r, c: (r, c ^ 1)))

    span = matrix.shape[1] // 2
    shares = [
        lax.ppermute(
            first[h * span : (h + 1) * span],
            both,
            pairs(lambda r, c, h=h: ((2 * c + h) ^ r, r), NB),
        )
        for h in range(2)
    ]
    odd = (col % 2).astype(jnp.int32).reshape(1)
    state = factor_call(start_kernel, (odd,), (own, other), {}, 3)
    shares, state = lax.optimization_barrier((shares, state))
    share = jnp.where((row ^ col) % 2 == 0, shares[0], shares[1])
    partner_cols = lax.all_to_all(
        jnp.broadcast_to(share[None], (rows,) + share.shape), "row", 0, 0
    )
    work, diag, _, _ = factor_call(finish_kernel, (), state, {i: i for i in range(4)}, 4)
    panel, schur = tail(place, pattern, panel_cols, partner_cols, matrix, work, diag)
    return (panel, schur)


def solution(mesh):
    in_specs = (P("row", "col"), P())
    out_specs = (P("row", None), P("row", "col"))
    return jax.shard_map(
        on_device, mesh=mesh, in_specs=in_specs, out_specs=out_specs, check_vma=False
    )
```

```python
import jax
import jax.numpy as jnp
from jax import lax
from jax.experimental import pallas as pl
from jax.experimental.pallas import tpu as pltpu
from jax.sharding import PartitionSpec as P

BLK = 128
PB = 4
NB = 2 * PB
PW = NB * BLK
SUB = 16
SLOTS = 3
HOLD = [
    [[0, 2, 4], [1]],
    [[2, 6], [1, 3, 7]],
    [[2, 4, 6], [3, 5]],
    [[0, 4, 6], [3, 5]],
    [[4, 6], [1, 7]],
    [[0, 4], [1, 5]],
    [[0, 6], [5, 7]],
    [[0, 2], [3, 5, 7]],
]


def split(x):
    high = x.astype(jnp.bfloat16)
    return high, (x - high.astype(jnp.float32)).astype(jnp.bfloat16)


def split3(x):
    high = x.astype(jnp.bfloat16)
    rest = x - high.astype(jnp.float32)
    mid = rest.astype(jnp.bfloat16)
    return high, mid, (rest - mid.astype(jnp.float32)).astype(jnp.bfloat16)


def left6(x):
    high, mid, low = split3(x)
    return jnp.concatenate([high, mid, high, mid, high, low], axis=1)


def right6(x, axis):
    high, mid, low = split3(x)
    return jnp.concatenate([high, high, mid, mid, low, high], axis=axis)


def dot_nn(a, b):
    return jnp.dot(a, b, preferred_element_type=jnp.float32)


def dot_nt(a, b):
    return lax.dot_general(a, b, (((1,), (1,)), ((), ())), preferred_element_type=jnp.float32)


def lane_copy(x, lane):
    return jnp.broadcast_to(x[:, lane : lane + 1], (8, BLK))


def row_copy(x, row):
    return jnp.broadcast_to(x[row : row + 1, :], (8, BLK))


def reciprocal(x):
    return pl.reciprocal(x, approx=True)


def invert_base(tiles):
    sub = lax.broadcasted_iota(jnp.int32, (8, BLK), 0)
    lane = lax.broadcasted_iota(jnp.int32, (8, BLK), 1)
    tiles = list(tiles)
    result = []
    for panel in range(BLK // 8):
        c0 = panel * 8
        inside = (lane >= c0) & (lane < c0 + 8)
        cols = [lane_copy(tiles[panel], c0 + k) for k in range(8)]
        rows = jnp.where(inside, jnp.where(lane == sub + c0, 1.0, 0.0), tiles[panel])
        upper = rows
        pivots = jnp.ones((8, BLK), jnp.float32)
        for p in range(0, 8, 2):
            one, two = sub == p, sub == p + 1
            pair = one | two
            a, b = row_copy(cols[p], p), row_copy(cols[p + 1], p)
            c = row_copy(cols[p + 1], p + 1)
            det = a * c - b * b
            inv_det, inv_a = reciprocal(det), reciprocal(a)
            aa, ab, bb = c * inv_det, b * inv_det, a * inv_det
            top, low = row_copy(rows, p), row_copy(rows, p + 1)
            pivots = jnp.where(one, a, jnp.where(two, det * inv_a, pivots))
            upper = jnp.where(one, top, jnp.where(two, low - b * inv_a * top, upper))

            def swept(x, y, target):
                u, v = aa * x - ab * y, bb * y - ab * x
                return jnp.where(pair, jnp.where(one, u, v), target - (cols[p] * u + cols[p + 1] * v))

            for k in range(p + 2, 8):
                cols[k] = swept(row_copy(cols[k], p), row_copy(cols[k], p + 1), cols[k])
            rows = swept(top, low, rows)
        result.append(jnp.where(lane <= sub + c0, upper * lax.rsqrt(pivots), 0.0))
        if panel < 15:
            solved = [row_copy(rows, k) for k in range(8)]
            for g in range(panel + 1, 16):
                parts = [lane_copy(tiles[g], c0 + k) * solved[k] for k in range(8)]
                while len(parts) > 1:
                    parts = [parts[m] + parts[m + 1] for m in range(0, len(parts), 2)]
                tiles[g] = jnp.where(inside, 0.0, tiles[g]) - parts[0]
    return result


def invert_into(base, block):
    for g, tile in enumerate(invert_base([block[8 * g : 8 * g + 8, :] for g in range(16)])):
        base[8 * g : 8 * g + 8, :] = tile


def lower_part(x):
    shape = (BLK, BLK)
    keep = lax.broadcasted_iota(jnp.int32, shape, 1) <= lax.broadcasted_iota(jnp.int32, shape, 0)
    return jnp.where(keep, x, 0.0)


def factor_steps(first, last, work, diag, head, base):
    def step(k, carry):
        here = pl.ds(pl.multiple_of(k * BLK, BLK), BLK)
        there = pl.ds(pl.multiple_of(k * BLK + BLK, BLK), BLK)
        inv, block = base[...], head[...]
        inv_left, inv_right = left6(inv), right6(inv, 1)
        below = dot_nt(left6(work[k + 1, :, here]), inv_right)
        beside = dot_nn(inv_left, right6(work[k, :, there], 0))
        following = work[k + 1, :, there] - dot_nn(left6(below), right6(beside, 0))
        head[...] = following
        tiles = invert_base([following[8 * g : 8 * g + 8, :] for g in range(16)])
        diag[k] = lower_part(dot_nt(left6(block), inv_right))
        work[k] = dot_nn(inv_left, right6(work[k], 0))
        work[k, :, here] = inv
        sweep = right6(work[k], 0)
        for i in range(first + 1, NB):
            block = work[i, :, here]
            below = left6(jnp.where(i > k, dot_nt(left6(block), inv_right), 0.0))
            work[i, :, here] = jnp.where(i > k, 0.0, block)
            work[i] = work[i] - dot_nn(below, sweep)
        for g in range(16):
            base[8 * g : 8 * g + 8, :] = tiles[g]
        return carry

    lax.fori_loop(first, last, step, 0)


FIRST_STEPS = 2


def start_kernel(odd_ref, own_ref, other_ref, work, diag, head, base):
    odd = odd_ref[0] == 1
    for i in range(NB):
        for parity in range(2):
            for slot, j in enumerate(HOLD[i][parity]):
                parts = []
                for at in (i, i + NB):
                    mine, theirs = own_ref[at, slot], other_ref[at, slot]
                    parts.append(jnp.where(odd == (parity == 1), mine, theirs))
                block = jnp.concatenate(parts, axis=0)
                work[i, :, j * BLK : (j + 1) * BLK] = block
                if i != j:
                    work[j, :, i * BLK : (i + 1) * BLK] = block.T
    head[...] = work[0, :, :BLK]
    invert_into(base, head)
    factor_steps(0, FIRST_STEPS, work, diag, head, base)


def finish_kernel(w_in, d_in, h_in, b_in, work, diag, head, base):
    factor_steps(FIRST_STEPS, NB - 1, work, diag, head, base)
    last = NB - 1
    inv = base[...]
    diag[last] = lower_part(dot_nt(left6(head[...]), right6(inv, 1)))
    work[last] = dot_nn(left6(inv), right6(work[last], 0))
    work[last, :, last * BLK :] = inv


STATE = [
    jax.ShapeDtypeStruct((NB, BLK, PW), jnp.float32),
    jax.ShapeDtypeStruct((NB, BLK, BLK), jnp.float32),
    jax.ShapeDtypeStruct((BLK, BLK), jnp.float32),
    jax.ShapeDtypeStruct((BLK, BLK), jnp.float32),
]


def factor_call(kernel, scalars, operands, aliases, share):
    vmem = pl.BlockSpec(memory_space=pltpu.VMEM)
    return pl.pallas_call(
        kernel,
        out_shape=STATE,
        in_specs=[pl.BlockSpec(memory_space=pltpu.SMEM)] * len(scalars) + [vmem] * len(operands),
        out_specs=[vmem] * len(STATE),
        input_output_aliases=aliases,
        compiler_params=pltpu.CompilerParams(vmem_limit_bytes=24 * 2**20),
        cost_estimate=pl.CostEstimate(
            flops=share * 10**10, bytes_accessed=share * 25 * 10**6, transcendentals=0
        ),
    )(*scalars, *operands)


def dot3(a, b):
    return dot_nt(
        jnp.concatenate([a[0], a[1], a[0]], axis=1), jnp.concatenate([b[0], b[0], b[1]], axis=1)
    )


TILE = 512
STEP = 256


def tail_kernel(
    at_ref, pattern_ref, w_ref, wq_ref, m_ref, work, diag, p_ref, s_ref, ah, al, qh, ql, vh, vl
):
    tile = pl.program_id(0)
    row, col = at_ref[0], at_ref[1]
    per = TILE // BLK

    def masked(j, first_block, owner, get):
        for b in range(per):
            entry = pattern_ref[j // PB, (first_block + b) * 16 + owner].astype(jnp.float32)
            high, low = split(get(j, b) * entry)
            ah[b * BLK : (b + 1) * BLK, j * BLK : (j + 1) * BLK] = high
            al[b * BLK : (b + 1) * BLK, j * BLK : (j + 1) * BLK] = low

    def solve(store):
        for n in range(PW // STEP):
            rows = slice(n * STEP, (n + 1) * STEP)
            depth = slice(0, (n + 1) * STEP)
            store(rows, dot3((ah[:, depth], al[:, depth]), (vh[rows, depth], vl[rows, depth])))

    @pl.when(tile == 0)
    def _():
        lane = lax.broadcasted_iota(jnp.int32, (BLK, PW), 1)
        for k in range(NB):
            high, low = split(jnp.where(lane < (k + 1) * BLK, work[k], 0.0))
            vh[k * BLK : (k + 1) * BLK, :] = high
            vl[k * BLK : (k + 1) * BLK, :] = low
        for h in range(qh.shape[0] // TILE):
            for j in range(NB):
                masked(
                    j,
                    per * h,
                    col,
                    lambda j, b: wq_ref[
                        (2 * j + (per * h + b) // 2) ^ col, b % 2 * BLK : (b % 2 + 1) * BLK, :
                    ],
                )

            def keep(cols, value):
                high, low = split(value)
                qh[h * TILE : (h + 1) * TILE, cols] = high
                ql[h * TILE : (h + 1) * TILE, cols] = low

            solve(keep)

    for j in range(NB):
        masked(j, per * tile, row, lambda j, b: w_ref[j, b * BLK : (b + 1) * BLK, :])

    def put(cols, value):
        p_ref[:, cols] = value

    solve(put)

    top = (tile == 0) & (row < NB)

    @pl.when(top)
    def _():
        here = pl.ds(pl.multiple_of(row * BLK, BLK), BLK)
        for k in range(NB):
            block = jnp.where(k < row, work[k, :, here].T, 0.0)
            p_ref[:BLK, k * BLK : (k + 1) * BLK] = jnp.where(k == row, diag[row], block)

    s_ref[...] = m_ref[...] - dot3(split(p_ref[...]), (qh[...], ql[...]))

    @pl.when(col < NB)
    def _():
        s_ref[:, :BLK] = jnp.zeros((TILE, BLK), jnp.float32)

    @pl.when(top)
    def _():
        s_ref[:BLK, :] = jnp.zeros((BLK, s_ref.shape[1]), jnp.float32)


def tail(at, pattern, panel_cols, partner_cols, matrix, work, diag):
    rows, width = matrix.shape
    grid_spec = pltpu.PrefetchScalarGridSpec(
        num_scalar_prefetch=2,
        grid=(rows // TILE,),
        in_specs=[
            pl.BlockSpec((NB, TILE, BLK), lambda t, *_: (0, t, 0)),
            pl.BlockSpec(memory_space=pltpu.VMEM),
            pl.BlockSpec((TILE, width), lambda t, *_: (t, 0)),
            pl.BlockSpec(memory_space=pltpu.VMEM),
            pl.BlockSpec(memory_space=pltpu.VMEM),
        ],
        out_specs=[
            pl.BlockSpec((TILE, PW), lambda t, *_: (t, 0)),
            pl.BlockSpec((TILE, width), lambda t, *_: (t, 0)),
        ],
        scratch_shapes=[
            pltpu.VMEM((TILE, PW), jnp.bfloat16),
            pltpu.VMEM((TILE, PW), jnp.bfloat16),
            pltpu.VMEM((width, PW), jnp.bfloat16),
            pltpu.VMEM((width, PW), jnp.bfloat16),
            pltpu.VMEM((PW, PW), jnp.bfloat16),
            pltpu.VMEM((PW, PW), jnp.bfloat16),
        ],
    )
    return pl.pallas_call(
        tail_kernel,
        grid_spec=grid_spec,
        out_shape=[
            jax.ShapeDtypeStruct((rows, PW), jnp.float32),
            jax.ShapeDtypeStruct((rows, width), jnp.float32),
        ],
        compiler_params=pltpu.CompilerParams(vmem_limit_bytes=44 * 2**20),
        cost_estimate=pl.CostEstimate(
            flops=10 * 10**9, bytes_accessed=20 * 10**6, transcendentals=0
        ),
    )(at, pattern, panel_cols, partner_cols, matrix, work, diag)


def pack_kernel(at_ref, corner_ref, out_ref):
    row, odd = at_ref[0] % NB, at_ref[1] % 2
    for i in range(NB):
        for parity in range(2):

            @pl.when((row == i) & (odd == parity))
            def _():
                for slot in range(SLOTS):
                    held = HOLD[i][parity]
                    block = corner_ref[held[min(slot, len(held) - 1)] // 2]
                    for target in range(out_ref.shape[0]):
                        out_ref[target, slot] = block


def pack(at, corner, rows):
    return pl.pallas_call(
        pack_kernel,
        out_shape=jax.ShapeDtypeStruct((rows, SLOTS) + corner.shape[1:], jnp.float32),
        in_specs=[
            pl.BlockSpec(memory_space=pltpu.SMEM),
            pl.BlockSpec(memory_space=pltpu.VMEM),
        ],
        out_specs=pl.BlockSpec(memory_space=pltpu.VMEM),
        compiler_params=pltpu.CompilerParams(vmem_limit_bytes=16 * 2**20),
    )(at, corner)


def on_device(matrix, pattern):
    rows = lax.axis_size("row")
    cols = lax.axis_size("col")
    row = lax.axis_index("row")
    col = lax.axis_index("col")
    both = ("row", "col")

    def at(r, c):
        return r * cols + c

    def pairs(target, width=cols):
        return [(at(r, c), at(*target(r, c))) for r in range(rows) for c in range(width)]

    first = matrix[:, :BLK]
    cut = BLK // 2
    groups = [
        [at(r + o, c) for o in (0, NB) for c in range(core, cols, 2)]
        for r in range(NB)
        for core in range(2)
    ]
    corner = jnp.repeat(first[:BLK].reshape(2, cut, BLK), cols // 2, axis=0)
    corner = lax.all_to_all(corner, both, 0, 0, axis_index_groups=groups)
    first, corner = lax.optimization_barrier((first, corner))

    place = jnp.stack([row, col]).astype(jnp.int32)

    panel_cols = lax.all_gather(first, "col", axis=0)

    own = lax.all_to_all(pack(place, corner, rows), "row", 0, 0)
    first, own = lax.optimization_barrier((first, own))
    other = lax.ppermute(own, both, pairs(lambda r, c: (r, c ^ 1)))

    span = matrix.shape[1] // 2
    shares = [
        lax.ppermute(
            first[h * span : (h + 1) * span],
            both,
            pairs(lambda r, c, h=h: ((2 * c + h) ^ r, r), NB),
        )
        for h in range(2)
    ]
    odd = (col % 2).astype(jnp.int32).reshape(1)
    state = factor_call(start_kernel, (odd,), (own, other), {}, 3)
    shares, state = lax.optimization_barrier((shares, state))
    share = jnp.where((row ^ col) % 2 == 0, shares[0], shares[1])
    partner_cols = lax.all_to_all(
        jnp.broadcast_to(share[None], (rows,) + share.shape), "row", 0, 0
    )
    work, diag, _, _ = factor_call(finish_kernel, (), state, {i: i for i in range(4)}, 4)
    panel, schur = tail(place, pattern, panel_cols, partner_cols, matrix, work, diag)
    return (panel, schur)


def solution(mesh):
    in_specs = (P("row", "col"), P())
    out_specs = (P("row", None), P("row", "col"))
    return jax.shard_map(
        on_device, mesh=mesh, in_specs=in_specs, out_specs=out_specs, check_vma=False
    )
```

```python
import jax
import jax.numpy as jnp
from jax import lax
from jax.experimental import pallas as pl
from jax.experimental.pallas import tpu as pltpu
from jax.sharding import PartitionSpec as P

BLK = 128
PB = 4
NB = 2 * PB
PW = NB * BLK
SUB = 16
SLOTS = 3
HOLD = [
    [[0, 2, 4], [1]],
    [[2, 6], [1, 3, 7]],
    [[2, 4, 6], [3, 5]],
    [[0, 4, 6], [3, 5]],
    [[4, 6], [1, 7]],
    [[0, 4], [1, 5]],
    [[0, 6], [5, 7]],
    [[0, 2], [3, 5, 7]],
]


def split(x):
    high = x.astype(jnp.bfloat16)
    return high, (x - high.astype(jnp.float32)).astype(jnp.bfloat16)


def split3(x):
    high = x.astype(jnp.bfloat16)
    rest = x - high.astype(jnp.float32)
    mid = rest.astype(jnp.bfloat16)
    return high, mid, (rest - mid.astype(jnp.float32)).astype(jnp.bfloat16)


def left6(x):
    high, mid, low = split3(x)
    return jnp.concatenate([high, mid, high, mid, high, low], axis=1)


def right6(x, axis):
    high, mid, low = split3(x)
    return jnp.concatenate([high, high, mid, mid, low, high], axis=axis)


def dot_nn(a, b):
    return jnp.dot(a, b, preferred_element_type=jnp.float32)


def dot_nt(a, b):
    return lax.dot_general(a, b, (((1,), (1,)), ((), ())), preferred_element_type=jnp.float32)


def lane_copy(x, lane):
    return jnp.broadcast_to(x[:, lane : lane + 1], (8, BLK))


def row_copy(x, row):
    return jnp.broadcast_to(x[row : row + 1, :], (8, BLK))


def reciprocal(x):
    return pl.reciprocal(x, approx=True)


def invert_base(tiles):
    sub = lax.broadcasted_iota(jnp.int32, (8, BLK), 0)
    lane = lax.broadcasted_iota(jnp.int32, (8, BLK), 1)
    tiles = list(tiles)
    result = []
    for panel in range(BLK // 8):
        c0 = panel * 8
        inside = (lane >= c0) & (lane < c0 + 8)
        cols = [lane_copy(tiles[panel], c0 + k) for k in range(8)]
        rows = jnp.where(inside, jnp.where(lane == sub + c0, 1.0, 0.0), tiles[panel])
        upper = rows
        pivots = jnp.ones((8, BLK), jnp.float32)
        for p in range(0, 8, 2):
            one, two = sub == p, sub == p + 1
            pair = one | two
            a, b = row_copy(cols[p], p), row_copy(cols[p + 1], p)
            c = row_copy(cols[p + 1], p + 1)
            det = a * c - b * b
            inv_det, inv_a = reciprocal(det), reciprocal(a)
            aa, ab, bb = c * inv_det, b * inv_det, a * inv_det
            top, low = row_copy(rows, p), row_copy(rows, p + 1)
            pivots = jnp.where(one, a, jnp.where(two, det * inv_a, pivots))
            upper = jnp.where(one, top, jnp.where(two, low - b * inv_a * top, upper))

            def swept(x, y, target):
                u, v = aa * x - ab * y, bb * y - ab * x
                return jnp.where(pair, jnp.where(one, u, v), target - (cols[p] * u + cols[p + 1] * v))

            for k in range(p + 2, 8):
                cols[k] = swept(row_copy(cols[k], p), row_copy(cols[k], p + 1), cols[k])
            rows = swept(top, low, rows)
        result.append(jnp.where(lane <= sub + c0, upper * lax.rsqrt(pivots), 0.0))
        if panel < 15:
            solved = [row_copy(rows, k) for k in range(8)]
            for g in range(panel + 1, 16):
                parts = [lane_copy(tiles[g], c0 + k) * solved[k] for k in range(8)]
                while len(parts) > 1:
                    parts = [parts[m] + parts[m + 1] for m in range(0, len(parts), 2)]
                tiles[g] = jnp.where(inside, 0.0, tiles[g]) - parts[0]
    return result


def invert_into(base, block):
    for g, tile in enumerate(invert_base([block[8 * g : 8 * g + 8, :] for g in range(16)])):
        base[8 * g : 8 * g + 8, :] = tile


def lower_part(x):
    shape = (BLK, BLK)
    keep = lax.broadcasted_iota(jnp.int32, shape, 1) <= lax.broadcasted_iota(jnp.int32, shape, 0)
    return jnp.where(keep, x, 0.0)


def factor_steps(first, last, work, diag, head, base):
    def step(k, carry):
        here = pl.ds(pl.multiple_of(k * BLK, BLK), BLK)
        there = pl.ds(pl.multiple_of(k * BLK + BLK, BLK), BLK)
        inv, block = base[...], head[...]
        inv_left, inv_right = left6(inv), right6(inv, 1)
        below = dot_nt(left6(work[k + 1, :, here]), inv_right)
        beside = dot_nn(inv_left, right6(work[k, :, there], 0))
        following = work[k + 1, :, there] - dot_nn(left6(below), right6(beside, 0))
        head[...] = following
        tiles = invert_base([following[8 * g : 8 * g + 8, :] for g in range(16)])
        diag[k] = lower_part(dot_nt(left6(block), inv_right))
        work[k] = dot_nn(inv_left, right6(work[k], 0))
        work[k, :, here] = inv
        sweep = right6(work[k], 0)
        for i in range(first + 1, NB):
            block = work[i, :, here]
            below = left6(jnp.where(i > k, dot_nt(left6(block), inv_right), 0.0))
            work[i, :, here] = jnp.where(i > k, 0.0, block)
            work[i] = work[i] - dot_nn(below, sweep)
        for g in range(16):
            base[8 * g : 8 * g + 8, :] = tiles[g]
        return carry

    lax.fori_loop(first, last, step, 0)


FIRST_STEPS = 2


def start_kernel(odd_ref, own_ref, other_ref, work, diag, head, base):
    odd = odd_ref[0] == 1
    for i in range(NB):
        for parity in range(2):
            for slot, j in enumerate(HOLD[i][parity]):
                parts = []
                for at in (i, i + NB):
                    mine, theirs = own_ref[at, slot], other_ref[at, slot]
                    parts.append(jnp.where(odd == (parity == 1), mine, theirs))
                block = jnp.concatenate(parts, axis=0)
                work[i, :, j * BLK : (j + 1) * BLK] = block
                if i != j:
                    work[j, :, i * BLK : (i + 1) * BLK] = block.T
    head[...] = work[0, :, :BLK]
    invert_into(base, head)
    factor_steps(0, FIRST_STEPS, work, diag, head, base)


def finish_kernel(w_in, d_in, h_in, b_in, work, diag, head, base):
    factor_steps(FIRST_STEPS, NB - 1, work, diag, head, base)
    last = NB - 1
    inv = base[...]
    diag[last] = lower_part(dot_nt(left6(head[...]), right6(inv, 1)))
    work[last] = dot_nn(left6(inv), right6(work[last], 0))
    work[last, :, last * BLK :] = inv


STATE = [
    jax.ShapeDtypeStruct((NB, BLK, PW), jnp.float32),
    jax.ShapeDtypeStruct((NB, BLK, BLK), jnp.float32),
    jax.ShapeDtypeStruct((BLK, BLK), jnp.float32),
    jax.ShapeDtypeStruct((BLK, BLK), jnp.float32),
]


def factor_call(kernel, scalars, operands, aliases, share):
    vmem = pl.BlockSpec(memory_space=pltpu.VMEM)
    return pl.pallas_call(
        kernel,
        out_shape=STATE,
        in_specs=[pl.BlockSpec(memory_space=pltpu.SMEM)] * len(scalars) + [vmem] * len(operands),
        out_specs=[vmem] * len(STATE),
        input_output_aliases=aliases,
        compiler_params=pltpu.CompilerParams(vmem_limit_bytes=24 * 2**20),
        cost_estimate=pl.CostEstimate(
            flops=share * 10**10, bytes_accessed=share * 25 * 10**6, transcendentals=0
        ),
    )(*scalars, *operands)


def dot3(a, b):
    return dot_nt(
        jnp.concatenate([a[0], a[1], a[0]], axis=1), jnp.concatenate([b[0], b[0], b[1]], axis=1)
    )


TILE = 512
STEP = 256


def tail_kernel(
    at_ref, pattern_ref, w_ref, wq_ref, m_ref, work, diag, p_ref, s_ref, ah, al, qh, ql, vh, vl
):
    tile = pl.program_id(0)
    row, col = at_ref[0], at_ref[1]
    per = TILE // BLK

    def masked(j, first_block, owner, get):
        for b in range(per):
            entry = pattern_ref[j // PB, (first_block + b) * 16 + owner].astype(jnp.float32)
            high, low = split(get(j, b) * entry)
            ah[b * BLK : (b + 1) * BLK, j * BLK : (j + 1) * BLK] = high
            al[b * BLK : (b + 1) * BLK, j * BLK : (j + 1) * BLK] = low

    def solve(store):
        for n in range(PW // STEP):
            rows = slice(n * STEP, (n + 1) * STEP)
            depth = slice(0, (n + 1) * STEP)
            store(rows, dot3((ah[:, depth], al[:, depth]), (vh[rows, depth], vl[rows, depth])))

    @pl.when(tile == 0)
    def _():
        lane = lax.broadcasted_iota(jnp.int32, (BLK, PW), 1)
        for k in range(NB):
            high, low = split(jnp.where(lane < (k + 1) * BLK, work[k], 0.0))
            vh[k * BLK : (k + 1) * BLK, :] = high
            vl[k * BLK : (k + 1) * BLK, :] = low
        for h in range(qh.shape[0] // TILE):
            for j in range(NB):
                masked(
                    j,
                    per * h,
                    col,
                    lambda j, b: wq_ref[
                        (2 * j + (per * h + b) // 2) ^ col, b % 2 * BLK : (b % 2 + 1) * BLK, :
                    ],
                )

            def keep(cols, value):
                high, low = split(value)
                qh[h * TILE : (h + 1) * TILE, cols] = high
                ql[h * TILE : (h + 1) * TILE, cols] = low

            solve(keep)

    for j in range(NB):
        masked(j, per * tile, row, lambda j, b: w_ref[j, b * BLK : (b + 1) * BLK, :])

    def put(cols, value):
        p_ref[:, cols] = value

    solve(put)

    top = (tile == 0) & (row < NB)

    @pl.when(top)
    def _():
        here = pl.ds(pl.multiple_of(row * BLK, BLK), BLK)
        for k in range(NB):
            block = jnp.where(k < row, work[k, :, here].T, 0.0)
            p_ref[:BLK, k * BLK : (k + 1) * BLK] = jnp.where(k == row, diag[row], block)

    s_ref[...] = m_ref[...] - dot3(split(p_ref[...]), (qh[...], ql[...]))

    @pl.when(col < NB)
    def _():
        s_ref[:, :BLK] = jnp.zeros((TILE, BLK), jnp.float32)

    @pl.when(top)
    def _():
        s_ref[:BLK, :] = jnp.zeros((BLK, s_ref.shape[1]), jnp.float32)


def tail(at, pattern, panel_cols, partner_cols, matrix, work, diag):
    rows, width = matrix.shape
    grid_spec = pltpu.PrefetchScalarGridSpec(
        num_scalar_prefetch=2,
        grid=(rows // TILE,),
        in_specs=[
            pl.BlockSpec((NB, TILE, BLK), lambda t, *_: (0, t, 0)),
            pl.BlockSpec(memory_space=pltpu.VMEM),
            pl.BlockSpec((TILE, width), lambda t, *_: (t, 0)),
            pl.BlockSpec(memory_space=pltpu.VMEM),
            pl.BlockSpec(memory_space=pltpu.VMEM),
        ],
        out_specs=[
            pl.BlockSpec((TILE, PW), lambda t, *_: (t, 0)),
            pl.BlockSpec((TILE, width), lambda t, *_: (t, 0)),
        ],
        scratch_shapes=[
            pltpu.VMEM((TILE, PW), jnp.bfloat16),
            pltpu.VMEM((TILE, PW), jnp.bfloat16),
            pltpu.VMEM((width, PW), jnp.bfloat16),
            pltpu.VMEM((width, PW), jnp.bfloat16),
            pltpu.VMEM((PW, PW), jnp.bfloat16),
            pltpu.VMEM((PW, PW), jnp.bfloat16),
        ],
    )
    return pl.pallas_call(
        tail_kernel,
        grid_spec=grid_spec,
        out_shape=[
            jax.ShapeDtypeStruct((rows, PW), jnp.float32),
            jax.ShapeDtypeStruct((rows, width), jnp.float32),
        ],
        compiler_params=pltpu.CompilerParams(vmem_limit_bytes=44 * 2**20),
        cost_estimate=pl.CostEstimate(
            flops=10 * 10**9, bytes_accessed=20 * 10**6, transcendentals=0
        ),
    )(at, pattern, panel_cols, partner_cols, matrix, work, diag)


def pack_kernel(at_ref, corner_ref, out_ref):
    row, odd = at_ref[0] % NB, at_ref[1] % 2
    for i in range(NB):
        for parity in range(2):

            @pl.when((row == i) & (odd == parity))
            def _():
                for slot in range(SLOTS):
                    held = HOLD[i][parity]
                    block = corner_ref[held[min(slot, len(held) - 1)] // 2]
                    for target in range(out_ref.shape[0]):
                        out_ref[target, slot] = block


def pack(at, corner, rows):
    return pl.pallas_call(
        pack_kernel,
        out_shape=jax.ShapeDtypeStruct((rows, SLOTS) + corner.shape[1:], jnp.float32),
        in_specs=[
            pl.BlockSpec(memory_space=pltpu.SMEM),
            pl.BlockSpec(memory_space=pltpu.VMEM),
        ],
        out_specs=pl.BlockSpec(memory_space=pltpu.VMEM),
        compiler_params=pltpu.CompilerParams(vmem_limit_bytes=16 * 2**20),
    )(at, corner)


def on_device(matrix, pattern):
    rows = lax.axis_size("row")
    cols = lax.axis_size("col")
    row = lax.axis_index("row")
    col = lax.axis_index("col")
    both = ("row", "col")

    def at(r, c):
        return r * cols + c

    def pairs(target, width=cols):
        return [(at(r, c), at(*target(r, c))) for r in range(rows) for c in range(width)]

    first = matrix[:, :BLK]
    cut = BLK // 2
    groups = [
        [at(r + o, c) for o in (0, NB) for c in range(core, cols, 2)]
        for r in range(NB)
        for core in range(2)
    ]
    corner = jnp.repeat(first[:BLK].reshape(2, cut, BLK), cols // 2, axis=0)
    corner = lax.all_to_all(corner, both, 0, 0, axis_index_groups=groups)
    first, corner = lax.optimization_barrier((first, corner))

    place = jnp.stack([row, col]).astype(jnp.int32)

    own = lax.all_to_all(pack(place, corner, rows), "row", 0, 0)
    first, own = lax.optimization_barrier((first, own))
    other = lax.ppermute(own, both, pairs(lambda r, c: (r, c ^ 1)))

    panel_cols = lax.all_gather(first, "col", axis=0)

    span = matrix.shape[1] // 2
    shares = [
        lax.ppermute(
            first[h * span : (h + 1) * span],
            both,
            pairs(lambda r, c, h=h: ((2 * c + h) ^ r, r), NB),
        )
        for h in range(2)
    ]
    odd = (col % 2).astype(jnp.int32).reshape(1)
    state = factor_call(start_kernel, (odd,), (own, other), {}, 3)
    shares, state = lax.optimization_barrier((shares, state))
    share = jnp.where((row ^ col) % 2 == 0, shares[0], shares[1])
    partner_cols = lax.all_to_all(
        jnp.broadcast_to(share[None], (rows,) + share.shape), "row", 0, 0
    )
    work, diag, _, _ = factor_call(finish_kernel, (), state, {i: i for i in range(4)}, 4)
    panel, schur = tail(place, pattern, panel_cols, partner_cols, matrix, work, diag)
    return (panel, schur)


def solution(mesh):
    in_specs = (P("row", "col"), P())
    out_specs = (P("row", None), P("row", "col"))
    return jax.shard_map(
        on_device, mesh=mesh, in_specs=in_specs, out_specs=out_specs, check_vma=False
    )
```

```python
import jax
import jax.numpy as jnp
from jax import lax
from jax.experimental import pallas as pl
from jax.experimental.pallas import tpu as pltpu
from jax.sharding import PartitionSpec as P

BLK = 128
PB = 4
NB = 2 * PB
PW = NB * BLK
SUB = 16
SLOTS = 3
HOLD = [
    [[0, 2, 4], [1]],
    [[2, 6], [1, 3, 7]],
    [[2, 4, 6], [3, 5]],
    [[0, 4, 6], [3, 5]],
    [[4, 6], [1, 7]],
    [[0, 4], [1, 5]],
    [[0, 6], [5, 7]],
    [[0, 2], [3, 5, 7]],
]


def split(x):
    high = x.astype(jnp.bfloat16)
    return high, (x - high.astype(jnp.float32)).astype(jnp.bfloat16)


def split3(x):
    high = x.astype(jnp.bfloat16)
    rest = x - high.astype(jnp.float32)
    mid = rest.astype(jnp.bfloat16)
    return high, mid, (rest - mid.astype(jnp.float32)).astype(jnp.bfloat16)


def left6(x):
    high, mid, low = split3(x)
    return jnp.concatenate([high, mid, high, mid, high, low], axis=1)


def right6(x, axis):
    high, mid, low = split3(x)
    return jnp.concatenate([high, high, mid, mid, low, high], axis=axis)


def dot_nn(a, b):
    return jnp.dot(a, b, preferred_element_type=jnp.float32)


def dot_nt(a, b):
    return lax.dot_general(a, b, (((1,), (1,)), ((), ())), preferred_element_type=jnp.float32)


def lane_copy(x, lane):
    return jnp.broadcast_to(x[:, lane : lane + 1], (8, BLK))


def row_copy(x, row):
    return jnp.broadcast_to(x[row : row + 1, :], (8, BLK))


def reciprocal(x):
    return pl.reciprocal(x, approx=True)


def invert_base(tiles):
    sub = lax.broadcasted_iota(jnp.int32, (8, BLK), 0)
    lane = lax.broadcasted_iota(jnp.int32, (8, BLK), 1)
    tiles = list(tiles)
    result = []
    for panel in range(BLK // 8):
        c0 = panel * 8
        inside = (lane >= c0) & (lane < c0 + 8)
        cols = [lane_copy(tiles[panel], c0 + k) for k in range(8)]
        rows = jnp.where(inside, jnp.where(lane == sub + c0, 1.0, 0.0), tiles[panel])
        upper = rows
        pivots = jnp.ones((8, BLK), jnp.float32)
        for p in range(0, 8, 2):
            one, two = sub == p, sub == p + 1
            pair = one | two
            a, b = row_copy(cols[p], p), row_copy(cols[p + 1], p)
            c = row_copy(cols[p + 1], p + 1)
            det = a * c - b * b
            inv_det, inv_a = reciprocal(det), reciprocal(a)
            aa, ab, bb = c * inv_det, b * inv_det, a * inv_det
            top, low = row_copy(rows, p), row_copy(rows, p + 1)
            pivots = jnp.where(one, a, jnp.where(two, det * inv_a, pivots))
            upper = jnp.where(one, top, jnp.where(two, low - b * inv_a * top, upper))

            def swept(x, y, target):
                u, v = aa * x - ab * y, bb * y - ab * x
                return jnp.where(pair, jnp.where(one, u, v), target - (cols[p] * u + cols[p + 1] * v))

            for k in range(p + 2, 8):
                cols[k] = swept(row_copy(cols[k], p), row_copy(cols[k], p + 1), cols[k])
            rows = swept(top, low, rows)
        result.append(jnp.where(lane <= sub + c0, upper * lax.rsqrt(pivots), 0.0))
        if panel < 15:
            solved = [row_copy(rows, k) for k in range(8)]
            for g in range(panel + 1, 16):
                parts = [lane_copy(tiles[g], c0 + k) * solved[k] for k in range(8)]
                while len(parts) > 1:
                    parts = [parts[m] + parts[m + 1] for m in range(0, len(parts), 2)]
                tiles[g] = jnp.where(inside, 0.0, tiles[g]) - parts[0]
    return result


def invert_into(base, block):
    for g, tile in enumerate(invert_base([block[8 * g : 8 * g + 8, :] for g in range(16)])):
        base[8 * g : 8 * g + 8, :] = tile


def lower_part(x):
    shape = (BLK, BLK)
    keep = lax.broadcasted_iota(jnp.int32, shape, 1) <= lax.broadcasted_iota(jnp.int32, shape, 0)
    return jnp.where(keep, x, 0.0)


def factor_steps(first, last, work, diag, head, base):
    def step(k, carry):
        here = pl.ds(pl.multiple_of(k * BLK, BLK), BLK)
        there = pl.ds(pl.multiple_of(k * BLK + BLK, BLK), BLK)
        inv, block = base[...], head[...]
        inv_left, inv_right = left6(inv), right6(inv, 1)
        below = dot_nt(left6(work[k + 1, :, here]), inv_right)
        beside = dot_nn(inv_left, right6(work[k, :, there], 0))
        following = work[k + 1, :, there] - dot_nn(left6(below), right6(beside, 0))
        head[...] = following
        tiles = invert_base([following[8 * g : 8 * g + 8, :] for g in range(16)])
        diag[k] = lower_part(dot_nt(left6(block), inv_right))
        work[k] = dot_nn(inv_left, right6(work[k], 0))
        work[k, :, here] = inv
        sweep = right6(work[k], 0)
        for i in range(first + 1, NB):
            block = work[i, :, here]
            below = left6(jnp.where(i > k, dot_nt(left6(block), inv_right), 0.0))
            work[i, :, here] = jnp.where(i > k, 0.0, block)
            work[i] = work[i] - dot_nn(below, sweep)
        for g in range(16):
            base[8 * g : 8 * g + 8, :] = tiles[g]
        return carry

    lax.fori_loop(first, last, step, 0)


FIRST_STEPS = 3


def start_kernel(odd_ref, own_ref, other_ref, work, diag, head, base):
    odd = odd_ref[0] == 1
    for i in range(NB):
        for parity in range(2):
            for slot, j in enumerate(HOLD[i][parity]):
                parts = []
                for at in (i, i + NB):
                    mine, theirs = own_ref[at, slot], other_ref[at, slot]
                    parts.append(jnp.where(odd == (parity == 1), mine, theirs))
                block = jnp.concatenate(parts, axis=0)
                work[i, :, j * BLK : (j + 1) * BLK] = block
                if i != j:
                    work[j, :, i * BLK : (i + 1) * BLK] = block.T
    head[...] = work[0, :, :BLK]
    invert_into(base, head)
    factor_steps(0, FIRST_STEPS, work, diag, head, base)


def finish_kernel(w_in, d_in, h_in, b_in, work, diag, head, base):
    factor_steps(FIRST_STEPS, NB - 1, work, diag, head, base)
    last = NB - 1
    inv = base[...]
    diag[last] = lower_part(dot_nt(left6(head[...]), right6(inv, 1)))
    work[last] = dot_nn(left6(inv), right6(work[last], 0))
    work[last, :, last * BLK :] = inv


STATE = [
    jax.ShapeDtypeStruct((NB, BLK, PW), jnp.float32),
    jax.ShapeDtypeStruct((NB, BLK, BLK), jnp.float32),
    jax.ShapeDtypeStruct((BLK, BLK), jnp.float32),
    jax.ShapeDtypeStruct((BLK, BLK), jnp.float32),
]


def factor_call(kernel, scalars, operands, aliases, share):
    vmem = pl.BlockSpec(memory_space=pltpu.VMEM)
    return pl.pallas_call(
        kernel,
        out_shape=STATE,
        in_specs=[pl.BlockSpec(memory_space=pltpu.SMEM)] * len(scalars) + [vmem] * len(operands),
        out_specs=[vmem] * len(STATE),
        input_output_aliases=aliases,
        compiler_params=pltpu.CompilerParams(vmem_limit_bytes=24 * 2**20),
        cost_estimate=pl.CostEstimate(
            flops=share * 10**10, bytes_accessed=share * 25 * 10**6, transcendentals=0
        ),
    )(*scalars, *operands)


def dot3(a, b):
    return dot_nt(
        jnp.concatenate([a[0], a[1], a[0]], axis=1), jnp.concatenate([b[0], b[0], b[1]], axis=1)
    )


TILE = 512
STEP = 256


def tail_kernel(
    at_ref, pattern_ref, w_ref, wq_ref, m_ref, work, diag, p_ref, s_ref, ah, al, qh, ql, vh, vl
):
    tile = pl.program_id(0)
    row, col = at_ref[0], at_ref[1]
    per = TILE // BLK

    def masked(j, first_block, owner, get):
        for b in range(per):
            entry = pattern_ref[j // PB, (first_block + b) * 16 + owner].astype(jnp.float32)
            high, low = split(get(j, b) * entry)
            ah[b * BLK : (b + 1) * BLK, j * BLK : (j + 1) * BLK] = high
            al[b * BLK : (b + 1) * BLK, j * BLK : (j + 1) * BLK] = low

    def solve(store):
        for n in range(PW // STEP):
            rows = slice(n * STEP, (n + 1) * STEP)
            depth = slice(0, (n + 1) * STEP)
            store(rows, dot3((ah[:, depth], al[:, depth]), (vh[rows, depth], vl[rows, depth])))

    @pl.when(tile == 0)
    def _():
        lane = lax.broadcasted_iota(jnp.int32, (BLK, PW), 1)
        for k in range(NB):
            high, low = split(jnp.where(lane < (k + 1) * BLK, work[k], 0.0))
            vh[k * BLK : (k + 1) * BLK, :] = high
            vl[k * BLK : (k + 1) * BLK, :] = low
        for h in range(qh.shape[0] // TILE):
            for j in range(NB):
                masked(
                    j,
                    per * h,
                    col,
                    lambda j, b: wq_ref[
                        (2 * j + (per * h + b) // 2) ^ col, b % 2 * BLK : (b % 2 + 1) * BLK, :
                    ],
                )

            def keep(cols, value):
                high, low = split(value)
                qh[h * TILE : (h + 1) * TILE, cols] = high
                ql[h * TILE : (h + 1) * TILE, cols] = low

            solve(keep)

    for j in range(NB):
        masked(j, per * tile, row, lambda j, b: w_ref[j, b * BLK : (b + 1) * BLK, :])

    def put(cols, value):
        p_ref[:, cols] = value

    solve(put)

    top = (tile == 0) & (row < NB)

    @pl.when(top)
    def _():
        here = pl.ds(pl.multiple_of(row * BLK, BLK), BLK)
        for k in range(NB):
            block = jnp.where(k < row, work[k, :, here].T, 0.0)
            p_ref[:BLK, k * BLK : (k + 1) * BLK] = jnp.where(k == row, diag[row], block)

    s_ref[...] = m_ref[...] - dot3(split(p_ref[...]), (qh[...], ql[...]))

    @pl.when(col < NB)
    def _():
        s_ref[:, :BLK] = jnp.zeros((TILE, BLK), jnp.float32)

    @pl.when(top)
    def _():
        s_ref[:BLK, :] = jnp.zeros((BLK, s_ref.shape[1]), jnp.float32)


def tail(at, pattern, panel_cols, partner_cols, matrix, work, diag):
    rows, width = matrix.shape
    grid_spec = pltpu.PrefetchScalarGridSpec(
        num_scalar_prefetch=2,
        grid=(rows // TILE,),
        in_specs=[
            pl.BlockSpec((NB, TILE, BLK), lambda t, *_: (0, t, 0)),
            pl.BlockSpec(memory_space=pltpu.VMEM),
            pl.BlockSpec((TILE, width), lambda t, *_: (t, 0)),
            pl.BlockSpec(memory_space=pltpu.VMEM),
            pl.BlockSpec(memory_space=pltpu.VMEM),
        ],
        out_specs=[
            pl.BlockSpec((TILE, PW), lambda t, *_: (t, 0)),
            pl.BlockSpec((TILE, width), lambda t, *_: (t, 0)),
        ],
        scratch_shapes=[
            pltpu.VMEM((TILE, PW), jnp.bfloat16),
            pltpu.VMEM((TILE, PW), jnp.bfloat16),
            pltpu.VMEM((width, PW), jnp.bfloat16),
            pltpu.VMEM((width, PW), jnp.bfloat16),
            pltpu.VMEM((PW, PW), jnp.bfloat16),
            pltpu.VMEM((PW, PW), jnp.bfloat16),
        ],
    )
    return pl.pallas_call(
        tail_kernel,
        grid_spec=grid_spec,
        out_shape=[
            jax.ShapeDtypeStruct((rows, PW), jnp.float32),
            jax.ShapeDtypeStruct((rows, width), jnp.float32),
        ],
        compiler_params=pltpu.CompilerParams(vmem_limit_bytes=44 * 2**20),
        cost_estimate=pl.CostEstimate(
            flops=10 * 10**9, bytes_accessed=20 * 10**6, transcendentals=0
        ),
    )(at, pattern, panel_cols, partner_cols, matrix, work, diag)


def pack_kernel(at_ref, corner_ref, out_ref):
    row, odd = at_ref[0] % NB, at_ref[1] % 2
    for i in range(NB):
        for parity in range(2):

            @pl.when((row == i) & (odd == parity))
            def _():
                for slot in range(SLOTS):
                    held = HOLD[i][parity]
                    block = corner_ref[held[min(slot, len(held) - 1)] // 2]
                    for target in range(out_ref.shape[0]):
                        out_ref[target, slot] = block


def pack(at, corner, rows):
    return pl.pallas_call(
        pack_kernel,
        out_shape=jax.ShapeDtypeStruct((rows, SLOTS) + corner.shape[1:], jnp.float32),
        in_specs=[
            pl.BlockSpec(memory_space=pltpu.SMEM),
            pl.BlockSpec(memory_space=pltpu.VMEM),
        ],
        out_specs=pl.BlockSpec(memory_space=pltpu.VMEM),
        compiler_params=pltpu.CompilerParams(vmem_limit_bytes=16 * 2**20),
    )(at, corner)


def on_device(matrix, pattern):
    rows = lax.axis_size("row")
    cols = lax.axis_size("col")
    row = lax.axis_index("row")
    col = lax.axis_index("col")
    both = ("row", "col")

    def at(r, c):
        return r * cols + c

    def pairs(target, width=cols):
        return [(at(r, c), at(*target(r, c))) for r in range(rows) for c in range(width)]

    panel_cols = lax.all_gather(matrix[:, :BLK], "col", axis=0)

    first = matrix[:, :BLK]
    cut = BLK // 2
    groups = [
        [at(r + o, c) for o in (0, NB) for c in range(core, cols, 2)]
        for r in range(NB)
        for core in range(2)
    ]
    corner = jnp.repeat(first[:BLK].reshape(2, cut, BLK), cols // 2, axis=0)
    corner = lax.all_to_all(corner, both, 0, 0, axis_index_groups=groups)
    first, corner = lax.optimization_barrier((first, corner))

    place = jnp.stack([row, col]).astype(jnp.int32)

    own = lax.all_to_all(pack(place, corner, rows), "row", 0, 0)
    first, own = lax.optimization_barrier((first, own))
    other = lax.ppermute(own, both, pairs(lambda r, c: (r, c ^ 1)))

    span = matrix.shape[1] // 2
    shares = [
        lax.ppermute(
            first[h * span : (h + 1) * span],
            both,
            pairs(lambda r, c, h=h: ((2 * c + h) ^ r, r), NB),
        )
        for h in range(2)
    ]
    odd = (col % 2).astype(jnp.int32).reshape(1)
    state = factor_call(start_kernel, (odd,), (own, other), {}, 3)
    shares, state = lax.optimization_barrier((shares, state))
    share = jnp.where((row ^ col) % 2 == 0, shares[0], shares[1])
    partner_cols = lax.all_to_all(
        jnp.broadcast_to(share[None], (rows,) + share.shape), "row", 0, 0
    )
    work, diag, _, _ = factor_call(finish_kernel, (), state, {i: i for i in range(4)}, 4)
    panel, schur = tail(place, pattern, panel_cols, partner_cols, matrix, work, diag)
    return (panel, schur)


def solution(mesh):
    in_specs = (P("row", "col"), P())
    out_specs = (P("row", None), P("row", "col"))
    return jax.shard_map(
        on_device, mesh=mesh, in_specs=in_specs, out_specs=out_specs, check_vma=False
    )
```

```python
import jax
import jax.numpy as jnp
from jax import lax
from jax.experimental import pallas as pl
from jax.experimental.pallas import tpu as pltpu
from jax.sharding import PartitionSpec as P

BLK = 128
PB = 4
NB = 2 * PB
PW = NB * BLK
SUB = 16
SLOTS = 3
HOLD = [
    [[0, 2, 4], [1]],
    [[2, 6], [1, 3, 7]],
    [[2, 4, 6], [3, 5]],
    [[0, 4, 6], [3, 5]],
    [[4, 6], [1, 7]],
    [[0, 4], [1, 5]],
    [[0, 6], [5, 7]],
    [[0, 2], [3, 5, 7]],
]


def split(x):
    high = x.astype(jnp.bfloat16)
    return high, (x - high.astype(jnp.float32)).astype(jnp.bfloat16)


def split3(x):
    high = x.astype(jnp.bfloat16)
    rest = x - high.astype(jnp.float32)
    mid = rest.astype(jnp.bfloat16)
    return high, mid, (rest - mid.astype(jnp.float32)).astype(jnp.bfloat16)


def left6(x):
    high, mid, low = split3(x)
    return jnp.concatenate([high, mid, high, mid, high, low], axis=1)


def right6(x, axis):
    high, mid, low = split3(x)
    return jnp.concatenate([high, high, mid, mid, low, high], axis=axis)


def dot_nn(a, b):
    return jnp.dot(a, b, preferred_element_type=jnp.float32)


def dot_nt(a, b):
    return lax.dot_general(a, b, (((1,), (1,)), ((), ())), preferred_element_type=jnp.float32)


def lane_copy(x, lane):
    return jnp.broadcast_to(x[:, lane : lane + 1], (8, BLK))


def row_copy(x, row):
    return jnp.broadcast_to(x[row : row + 1, :], (8, BLK))


def reciprocal(x):
    return pl.reciprocal(x, approx=True)


def invert_base(tiles):
    sub = lax.broadcasted_iota(jnp.int32, (8, BLK), 0)
    lane = lax.broadcasted_iota(jnp.int32, (8, BLK), 1)
    tiles = list(tiles)
    result = []
    for panel in range(BLK // 8):
        c0 = panel * 8
        inside = (lane >= c0) & (lane < c0 + 8)
        cols = [lane_copy(tiles[panel], c0 + k) for k in range(8)]
        rows = jnp.where(inside, jnp.where(lane == sub + c0, 1.0, 0.0), tiles[panel])
        upper = rows
        pivots = jnp.ones((8, BLK), jnp.float32)
        for p in range(0, 8, 2):
            one, two = sub == p, sub == p + 1
            pair = one | two
            a, b = row_copy(cols[p], p), row_copy(cols[p + 1], p)
            c = row_copy(cols[p + 1], p + 1)
            det = a * c - b * b
            inv_det, inv_a = reciprocal(det), reciprocal(a)
            aa, ab, bb = c * inv_det, b * inv_det, a * inv_det
            top, low = row_copy(rows, p), row_copy(rows, p + 1)
            pivots = jnp.where(one, a, jnp.where(two, det * inv_a, pivots))
            upper = jnp.where(one, top, jnp.where(two, low - b * inv_a * top, upper))

            def swept(x, y, target):
                u, v = aa * x - ab * y, bb * y - ab * x
                return jnp.where(pair, jnp.where(one, u, v), target - (cols[p] * u + cols[p + 1] * v))

            for k in range(p + 2, 8):
                cols[k] = swept(row_copy(cols[k], p), row_copy(cols[k], p + 1), cols[k])
            rows = swept(top, low, rows)
        result.append(jnp.where(lane <= sub + c0, upper * lax.rsqrt(pivots), 0.0))
        if panel < 15:
            solved = [row_copy(rows, k) for k in range(8)]
            for g in range(panel + 1, 16):
                parts = [lane_copy(tiles[g], c0 + k) * solved[k] for k in range(8)]
                while len(parts) > 1:
                    parts = [parts[m] + parts[m + 1] for m in range(0, len(parts), 2)]
                tiles[g] = jnp.where(inside, 0.0, tiles[g]) - parts[0]
    return result


def invert_into(base, block):
    for g, tile in enumerate(invert_base([block[8 * g : 8 * g + 8, :] for g in range(16)])):
        base[8 * g : 8 * g + 8, :] = tile


def lower_part(x):
    shape = (BLK, BLK)
    keep = lax.broadcasted_iota(jnp.int32, shape, 1) <= lax.broadcasted_iota(jnp.int32, shape, 0)
    return jnp.where(keep, x, 0.0)


def factor_steps(first, last, work, diag, head, base):
    def step(k, carry):
        here = pl.ds(pl.multiple_of(k * BLK, BLK), BLK)
        there = pl.ds(pl.multiple_of(k * BLK + BLK, BLK), BLK)
        inv, block = base[...], head[...]
        inv_left, inv_right = left6(inv), right6(inv, 1)
        below = dot_nt(left6(work[k + 1, :, here]), inv_right)
        beside = dot_nn(inv_left, right6(work[k, :, there], 0))
        following = work[k + 1, :, there] - dot_nn(left6(below), right6(beside, 0))
        head[...] = following
        tiles = invert_base([following[8 * g : 8 * g + 8, :] for g in range(16)])
        diag[k] = lower_part(dot_nt(left6(block), inv_right))
        work[k] = dot_nn(inv_left, right6(work[k], 0))
        work[k, :, here] = inv
        sweep = right6(work[k], 0)
        for i in range(first + 1, NB):
            block = work[i, :, here]
            below = left6(jnp.where(i > k, dot_nt(left6(block), inv_right), 0.0))
            work[i, :, here] = jnp.where(i > k, 0.0, block)
            work[i] = work[i] - dot_nn(below, sweep)
        for g in range(16):
            base[8 * g : 8 * g + 8, :] = tiles[g]
        return carry

    lax.fori_loop(first, last, step, 0)


FIRST_STEPS = 2


def start_kernel(odd_ref, own_ref, other_ref, work, diag, head, base):
    odd = odd_ref[0] == 1
    for i in range(NB):
        for parity in range(2):
            for slot, j in enumerate(HOLD[i][parity]):
                parts = []
                for at in (i, i + NB):
                    mine, theirs = own_ref[at, slot], other_ref[at, slot]
                    parts.append(jnp.where(odd == (parity == 1), mine, theirs))
                block = jnp.concatenate(parts, axis=0)
                work[i, :, j * BLK : (j + 1) * BLK] = block
                if i != j:
                    work[j, :, i * BLK : (i + 1) * BLK] = block.T
    head[...] = work[0, :, :BLK]
    invert_into(base, head)
    factor_steps(0, FIRST_STEPS, work, diag, head, base)


def finish_kernel(w_in, d_in, h_in, b_in, work, diag, head, base):
    factor_steps(FIRST_STEPS, NB - 1, work, diag, head, base)
    last = NB - 1
    inv = base[...]
    diag[last] = lower_part(dot_nt(left6(head[...]), right6(inv, 1)))
    work[last] = dot_nn(left6(inv), right6(work[last], 0))
    work[last, :, last * BLK :] = inv


STATE = [
    jax.ShapeDtypeStruct((NB, BLK, PW), jnp.float32),
    jax.ShapeDtypeStruct((NB, BLK, BLK), jnp.float32),
    jax.ShapeDtypeStruct((BLK, BLK), jnp.float32),
    jax.ShapeDtypeStruct((BLK, BLK), jnp.float32),
]


def factor_call(kernel, scalars, operands, aliases, share):
    vmem = pl.BlockSpec(memory_space=pltpu.VMEM)
    return pl.pallas_call(
        kernel,
        out_shape=STATE,
        in_specs=[pl.BlockSpec(memory_space=pltpu.SMEM)] * len(scalars) + [vmem] * len(operands),
        out_specs=[vmem] * len(STATE),
        input_output_aliases=aliases,
        compiler_params=pltpu.CompilerParams(vmem_limit_bytes=24 * 2**20),
        cost_estimate=pl.CostEstimate(
            flops=share * 10**10, bytes_accessed=share * 25 * 10**6, transcendentals=0
        ),
    )(*scalars, *operands)


def dot3(a, b):
    return dot_nt(
        jnp.concatenate([a[0], a[1], a[0]], axis=1), jnp.concatenate([b[0], b[0], b[1]], axis=1)
    )


TILE = 256
STEP = 256


def tail_kernel(
    at_ref, pattern_ref, w_ref, wq_ref, m_ref, work, diag, p_ref, s_ref, ah, al, qh, ql, vh, vl
):
    tile = pl.program_id(0)
    row, col = at_ref[0], at_ref[1]
    per = TILE // BLK

    def masked(j, first_block, owner, get):
        for b in range(per):
            entry = pattern_ref[j // PB, (first_block + b) * 16 + owner].astype(jnp.float32)
            high, low = split(get(j, b) * entry)
            ah[b * BLK : (b + 1) * BLK, j * BLK : (j + 1) * BLK] = high
            al[b * BLK : (b + 1) * BLK, j * BLK : (j + 1) * BLK] = low

    def solve(store):
        for n in range(PW // STEP):
            rows = slice(n * STEP, (n + 1) * STEP)
            depth = slice(0, (n + 1) * STEP)
            store(rows, dot3((ah[:, depth], al[:, depth]), (vh[rows, depth], vl[rows, depth])))

    @pl.when(tile == 0)
    def _():
        lane = lax.broadcasted_iota(jnp.int32, (BLK, PW), 1)
        for k in range(NB):
            high, low = split(jnp.where(lane < (k + 1) * BLK, work[k], 0.0))
            vh[k * BLK : (k + 1) * BLK, :] = high
            vl[k * BLK : (k + 1) * BLK, :] = low
        for h in range(qh.shape[0] // TILE):
            for j in range(NB):
                masked(
                    j,
                    per * h,
                    col,
                    lambda j, b: wq_ref[
                        (2 * j + (per * h + b) // 2) ^ col, b % 2 * BLK : (b % 2 + 1) * BLK, :
                    ],
                )

            def keep(cols, value):
                high, low = split(value)
                qh[h * TILE : (h + 1) * TILE, cols] = high
                ql[h * TILE : (h + 1) * TILE, cols] = low

            solve(keep)

    for j in range(NB):
        masked(j, per * tile, row, lambda j, b: w_ref[j, b * BLK : (b + 1) * BLK, :])

    def put(cols, value):
        p_ref[:, cols] = value

    solve(put)

    top = (tile == 0) & (row < NB)

    @pl.when(top)
    def _():
        here = pl.ds(pl.multiple_of(row * BLK, BLK), BLK)
        for k in range(NB):
            block = jnp.where(k < row, work[k, :, here].T, 0.0)
            p_ref[:BLK, k * BLK : (k + 1) * BLK] = jnp.where(k == row, diag[row], block)

    s_ref[...] = m_ref[...] - dot3(split(p_ref[...]), (qh[...], ql[...]))

    @pl.when(col < NB)
    def _():
        s_ref[:, :BLK] = jnp.zeros((TILE, BLK), jnp.float32)

    @pl.when(top)
    def _():
        s_ref[:BLK, :] = jnp.zeros((BLK, s_ref.shape[1]), jnp.float32)


def tail(at, pattern, panel_cols, partner_cols, matrix, work, diag):
    rows, width = matrix.shape
    grid_spec = pltpu.PrefetchScalarGridSpec(
        num_scalar_prefetch=2,
        grid=(rows // TILE,),
        in_specs=[
            pl.BlockSpec((NB, TILE, BLK), lambda t, *_: (0, t, 0)),
            pl.BlockSpec(memory_space=pltpu.VMEM),
            pl.BlockSpec((TILE, width), lambda t, *_: (t, 0)),
            pl.BlockSpec(memory_space=pltpu.VMEM),
            pl.BlockSpec(memory_space=pltpu.VMEM),
        ],
        out_specs=[
            pl.BlockSpec((TILE, PW), lambda t, *_: (t, 0)),
            pl.BlockSpec((TILE, width), lambda t, *_: (t, 0)),
        ],
        scratch_shapes=[
            pltpu.VMEM((TILE, PW), jnp.bfloat16),
            pltpu.VMEM((TILE, PW), jnp.bfloat16),
            pltpu.VMEM((width, PW), jnp.bfloat16),
            pltpu.VMEM((width, PW), jnp.bfloat16),
            pltpu.VMEM((PW, PW), jnp.bfloat16),
            pltpu.VMEM((PW, PW), jnp.bfloat16),
        ],
    )
    return pl.pallas_call(
        tail_kernel,
        grid_spec=grid_spec,
        out_shape=[
            jax.ShapeDtypeStruct((rows, PW), jnp.float32),
            jax.ShapeDtypeStruct((rows, width), jnp.float32),
        ],
        compiler_params=pltpu.CompilerParams(vmem_limit_bytes=44 * 2**20),
        cost_estimate=pl.CostEstimate(
            flops=10 * 10**9, bytes_accessed=20 * 10**6, transcendentals=0
        ),
    )(at, pattern, panel_cols, partner_cols, matrix, work, diag)


def pack_kernel(at_ref, corner_ref, out_ref):
    row, odd = at_ref[0] % NB, at_ref[1] % 2
    for i in range(NB):
        for parity in range(2):

            @pl.when((row == i) & (odd == parity))
            def _():
                for slot in range(SLOTS):
                    held = HOLD[i][parity]
                    block = corner_ref[held[min(slot, len(held) - 1)] // 2]
                    for target in range(out_ref.shape[0]):
                        out_ref[target, slot] = block


def pack(at, corner, rows):
    return pl.pallas_call(
        pack_kernel,
        out_shape=jax.ShapeDtypeStruct((rows, SLOTS) + corner.shape[1:], jnp.float32),
        in_specs=[
            pl.BlockSpec(memory_space=pltpu.SMEM),
            pl.BlockSpec(memory_space=pltpu.VMEM),
        ],
        out_specs=pl.BlockSpec(memory_space=pltpu.VMEM),
        compiler_params=pltpu.CompilerParams(vmem_limit_bytes=16 * 2**20),
    )(at, corner)


def on_device(matrix, pattern):
    rows = lax.axis_size("row")
    cols = lax.axis_size("col")
    row = lax.axis_index("row")
    col = lax.axis_index("col")
    both = ("row", "col")

    def at(r, c):
        return r * cols + c

    def pairs(target, width=cols):
        return [(at(r, c), at(*target(r, c))) for r in range(rows) for c in range(width)]

    first = matrix[:, :BLK]
    cut = BLK // 2
    groups = [
        [at(r + o, c) for o in (0, NB) for c in range(core, cols, 2)]
        for r in range(NB)
        for core in range(2)
    ]
    corner = jnp.repeat(first[:BLK].reshape(2, cut, BLK), cols // 2, axis=0)
    corner = lax.all_to_all(corner, both, 0, 0, axis_index_groups=groups)
    first, corner = lax.optimization_barrier((first, corner))

    place = jnp.stack([row, col]).astype(jnp.int32)

    panel_cols = lax.all_gather(first, "col", axis=0)

    own = lax.all_to_all(pack(place, corner, rows), "row", 0, 0)
    first, own = lax.optimization_barrier((first, own))
    other = lax.ppermute(own, both, pairs(lambda r, c: (r, c ^ 1)))

    span = matrix.shape[1] // 2
    shares = [
        lax.ppermute(
            first[h * span : (h + 1) * span],
            both,
            pairs(lambda r, c, h=h: ((2 * c + h) ^ r, r), NB),
        )
        for h in range(2)
    ]
    odd = (col % 2).astype(jnp.int32).reshape(1)
    state = factor_call(start_kernel, (odd,), (own, other), {}, 3)
    shares, state = lax.optimization_barrier((shares, state))
    share = jnp.where((row ^ col) % 2 == 0, shares[0], shares[1])
    partner_cols = lax.all_to_all(
        jnp.broadcast_to(share[None], (rows,) + share.shape), "row", 0, 0
    )
    work, diag, _, _ = factor_call(finish_kernel, (), state, {i: i for i in range(4)}, 4)
    panel, schur = tail(place, pattern, panel_cols, partner_cols, matrix, work, diag)
    return (panel, schur)


def solution(mesh):
    in_specs = (P("row", "col"), P())
    out_specs = (P("row", None), P("row", "col"))
    return jax.shard_map(
        on_device, mesh=mesh, in_specs=in_specs, out_specs=out_specs, check_vma=False
    )
```
